256 devices in a mesh: seq: 16 (over y, x_hi, core), blk: 16 (over z, x_lo).
Axes of the slice: x: 4 (x_hi: 2, x_lo: 2; x = x_hi * 2 + x_lo), y: 4, z: 8, core: 2. Of those that a mesh axis runs over, the one named last changes fastest.
Arguments:
- hidden_states: bfloat16 [16384, 4096], P(('seq', 'blk')), may hold values from -6 to 6
- query_weight: bfloat16 [4096, 4096], P(None, 'blk'), may hold values from -7.8125 to 7.8125
- kv_weight: bfloat16 [896, 2, 4096], P(None, None, 'blk'), may hold values from -0.1875 to 0.1875
- output_weight: bfloat16 [4096, 4096], P('blk'), may hold values from -0.09375 to 0.09375
- enc_in_weight: bfloat16 [3584, 896], P('blk'), may hold values from -0.1875 to 0.1875
- enc_out_weight: bfloat16 [3584, 896], P('blk'), may hold values from -0.09375 to 0.09375
- neighbours: bfloat16 [128, 768, 896], P('blk', 'seq'), may hold values from -6 to 6
- counts: int32 [16], replicated, may hold values from 1 to 48, 512 in all
- slot_of: int32 [512], replicated, may hold values from 0 to 511, as said below
Outputs:
- output: bfloat16 [16384, 4096], P(('seq', 'blk'))
The draws below stay inside these ranges and needn't reach their ends.
Inputs may be any that keep to these rules, and one draw needn't show every extreme that they name: counts sum to 512 and the largest is exactly 48. slot_of is a permutation; the neighbours kept by one holder fill at most 3 slots of any one index of seq, and some holder reaches 3; each index of seq owns 32 slots.
All inputs are finite; a program needn't handle non-finite values.
Results may differ from the reference program's by a relative error of at most 0.027.
The reference program's roundings to bfloat16 on the way count: a program that leaves them out, or rounds other values in their place, can miss the bound.
Values may be sent and summed in bfloat16 or wider, within the bound.
No kernel may reach another device: no remote copies, remote signals or barrier semaphores. Data moves between devices by JAX's collectives and lax.ppermute only.
A program may use at most 128 MiB of HBM per device.

```python
import math
import jax
import jax.numpy as jnp
import numpy as np
from jax import lax

D = 4096
HD = 128
HEADS_DEV = 2
DE = 896
FFE = 3584
NT = 128
CT = 64
K_NB = 2
CH_DEV = 16
HEADS = 32
HQ = 4096
SLOTS = 32
CAP = 48
NBR_TOTAL = 512
TOKENS = 16384
N_SEQ = 16
N_BLK = 16


def draw_query_weight(key, part):
    key = jax.random.fold_in(key, 3)
    base_key, head_key = jax.random.split(key)
    values = jnp.clip(jax.random.normal(base_key, (D, HEADS * HD), jnp.float32), -5.0, 5.0) * D ** (-0.5)
    spread = jnp.exp(jax.random.uniform(head_key, (HEADS,), jnp.float32, math.log(0.5), math.log(2.0)))
    return (values * jnp.repeat(spread, HD)[None, :]).astype(jnp.bfloat16)


def draw_slot_of(key, part):
    key = jax.random.fold_in(key, 7)
    owner_key, slot_key = jax.random.split(key)
    owners = jax.random.permutation(owner_key, N_SEQ).astype(jnp.int32)
    numbers = jnp.arange(NBR_TOTAL, dtype=jnp.int32)
    owner_of = owners[numbers % N_SEQ]
    slot_keys = jax.random.split(slot_key, N_SEQ)
    shuffles = jax.vmap(lambda subkey: jax.random.permutation(subkey, SLOTS))(slot_keys).astype(jnp.int32)
    position = shuffles[owner_of, numbers // N_SEQ]
    return (owner_of * SLOTS + position).astype(jnp.int32)


def levels(stream_key, shape, shards, least, high):
    def one(dim, shards_of):
        heights = jax.random.uniform(jax.random.fold_in(jax.random.fold_in(stream_key, 6), dim), (shards_of,), jnp.float32, least / len(shards), high / len(shards))
        return jnp.repeat(jnp.exp(heights), shape[dim] // shards_of).reshape((-1,) + (1,) * (len(shape) - dim - 1))

    loudness = one(*shards[0])
    for cut in shards[1:]:
        loudness = loudness * one(*cut)
    return loudness


def length_profile(amount, total, most, slope):
    portions = [(1 << 20) // math.isqrt(rank ** slope) + 1 for rank in range(2, amount + 1)]
    spare, given = total - most - (amount - 1), [1] * (amount - 1)
    while spare > 0:
        free = [i for i in range(amount - 1) if given[i] < most]
        whole, left = sum([portions[i] for i in free]), spare
        for i in free:
            more = min(most - given[i], max(1, left * portions[i] // whole), spare)
            given[i] = given[i] + more
            spare = spare - more
    return np.array([most] + given)


def uneven_parts(own_key, amount, total, limit, lean):
    if amount == 2:
        one = jax.random.randint(own_key, (), max(1, total - limit), min(limit, total - 1) + 1)
        return jnp.stack([one, total - one])
    tallies = jnp.asarray(length_profile(amount, total, limit, lean), jnp.int32)
    pairs = (amount - 1) // 2
    giver, receiver = tallies[1:1 + 2 * pairs:2], tallies[2:2 + 2 * pairs:2]
    room = jnp.minimum(giver - 1, limit - receiver)
    passed = jax.random.randint(jax.random.fold_in(own_key, 1), (pairs,), 0, 1 << 20) % (room + 1)
    tallies = tallies.at[1:1 + 2 * pairs:2].set(giver - passed).at[2:2 + 2 * pairs:2].set(receiver + passed)
    return tallies[jax.random.permutation(jax.random.fold_in(own_key, 2), amount)]


def centred(rng, extent, scale, reach, shards=(), kind=jnp.bfloat16):
    gain = levels(rng, extent, shards, -0.22, 0.18) if shards else 1.0
    result = jax.random.normal(rng, extent, jnp.float32) * scale * gain
    return jnp.minimum(jnp.maximum(result, -reach), reach).astype(kind)


def setup_inputs(seed: int = 0) -> dict:
    streams_of = jax.random.split(jax.random.key(seed), 10)
    return {
        "hidden_states": centred(streams_of[0], (TOKENS, D), 1.0, 6.0, ((0, 256),)),
        "query_weight": draw_query_weight(jax.random.fold_in(streams_of[9], 71), 0),
        "kv_weight": centred(streams_of[2], (DE, 2, HQ), DE ** -0.5, 0.1875, ((2, 16),)),
        "output_weight": centred(streams_of[3], (HQ, D), HQ ** -0.5, 0.09375, ((0, 16),)),
        "enc_in_weight": centred(streams_of[4], (FFE, DE), DE ** -0.5, 0.1875, ((0, 16),)),
        "enc_out_weight": centred(streams_of[5], (FFE, DE), FFE ** -0.5, 0.09375, ((0, 16),)),
        "neighbours": centred(streams_of[6], (NT, N_SEQ * CAP, DE), 1.0, 6.0, ((0, 16), (1, 16))),
        "counts": uneven_parts(streams_of[7], N_SEQ, NBR_TOTAL, CAP, 2).astype(jnp.int32),
        "slot_of": draw_slot_of(jax.random.fold_in(streams_of[9], 71), 0),
    }


epsilon = 1e-06

def rms_normed(rows):
    widened = rows.astype(jnp.float32)
    inv_rms = lax.rsqrt(lax.optimization_barrier(jnp.mean(widened * widened, axis=-1, keepdims=True)) + epsilon)
    return (widened * inv_rms).astype(jnp.bfloat16)

def encode_rows(raw_rows, enc_in_weight, enc_out_weight):
    normed = rms_normed(raw_rows)
    hidden = lax.dot_general(normed, enc_in_weight, (((1,), (1,)), ((), ())), preferred_element_type=jnp.float32)
    hidden = jax.nn.gelu(hidden, approximate=False).astype(jnp.bfloat16)
    summed = jnp.dot(hidden, enc_out_weight, preferred_element_type=jnp.float32)
    return (raw_rows.astype(jnp.float32) + summed).astype(jnp.bfloat16)

def reference(hidden_states, query_weight, kv_weight, output_weight, enc_in_weight, enc_out_weight, neighbours, counts, slot_of):
    numbers = jnp.arange(NBR_TOTAL, dtype=jnp.int32)
    run_ends = jnp.cumsum(counts).astype(jnp.int32)
    starts = (run_ends - counts).astype(jnp.int32)
    sender = lax.optimization_barrier(jnp.sum((run_ends[None, :] <= numbers[:, None]).astype(jnp.int32), axis=1)).astype(jnp.int32)
    source = (sender * CAP + numbers - starts[sender]).astype(jnp.int32)
    column_of = jnp.zeros((NBR_TOTAL,), jnp.int32).at[slot_of].set(source)
    gathered = jnp.take(neighbours, column_of, axis=1)
    per_owner = gathered.reshape(NT, N_SEQ, SLOTS, DE).transpose(1, 0, 2, 3)
    token_rows = hidden_states.reshape(N_SEQ, CH_DEV * CT, D)
    kv_flat = kv_weight.reshape(DE, 2 * HQ)
    out_groups = output_weight.reshape(N_BLK, HEADS_DEV * HD, D)

    def one_owner(operands):
        raw_rows, tokens = operands
        encoded = encode_rows(raw_rows.reshape(NT * SLOTS, DE), enc_in_weight, enc_out_weight)
        keyvals = jnp.dot(encoded, kv_flat, preferred_element_type=jnp.float32).astype(jnp.bfloat16)
        keyvals = keyvals.reshape(NT, CH_DEV, K_NB, 2, HEADS, HD).astype(jnp.float32)
        queries = (jnp.dot(rms_normed(tokens), query_weight, preferred_element_type=jnp.float32) * HD ** (-0.5)).astype(jnp.bfloat16)
        grouped_q = queries.reshape(CH_DEV, CT, HEADS, HD).astype(jnp.float32)
        scores = jnp.einsum('cqhe,tcnhe->chqtn', grouped_q, keyvals[:, :, :, 0])
        scores = scores.reshape(CH_DEV, HEADS, CT, NT * K_NB)
        row_max = lax.optimization_barrier(jnp.max(scores, axis=-1, keepdims=True))
        exponent = jnp.exp(scores - row_max)
        attn_probs = (exponent / lax.optimization_barrier(jnp.sum(exponent, axis=-1, keepdims=True))).astype(jnp.bfloat16)
        attn_probs = attn_probs.reshape(CH_DEV, HEADS, CT, NT, K_NB).astype(jnp.float32)
        mixed_heads = jnp.einsum('chqtn,tcnhe->cqhe', attn_probs, keyvals[:, :, :, 1]).astype(jnp.bfloat16)
        mixed_heads = mixed_heads.reshape(CH_DEV * CT, N_BLK, HEADS_DEV * HD).transpose(1, 0, 2)

        def accumulate(running, operands_two):
            part_sum = jnp.dot(operands_two[0], operands_two[1], preferred_element_type=jnp.float32)
            rounded = lax.optimization_barrier(part_sum.astype(jnp.bfloat16))
            return (running + rounded.astype(jnp.float32), None)
        summed, _ = lax.scan(accumulate, jnp.zeros((CH_DEV * CT, D), jnp.float32), (mixed_heads, out_groups))
        return (tokens.astype(jnp.float32) + summed).astype(jnp.bfloat16)
    results = lax.map(one_owner, (per_owner, token_rows))
    return results.reshape(TOKENS, D)
```

```python
import jax
import jax.numpy as jnp
from jax import lax
from jax.sharding import Mesh, PartitionSpec as P

HD = 128
CT = 64
K_NB = 2
EPS = 1e-06
AXES = ("y", "xh", "core", "z", "xl")
SIZES = (4, 2, 2, 8, 2)


def coords_of(index):
    out = []
    for size in reversed(SIZES):
        out.append(index % size)
        index //= size
    return tuple(reversed(out))


def index_of(coords):
    index = 0
    for size, coord in zip(SIZES, coords):
        index = index * size + coord % size
    return index


def pairs(target):
    count = index_of(tuple(s - 1 for s in SIZES)) + 1
    return [(i, index_of(target(*coords_of(i)))) for i in range(count)]


def x_shift(y, xh, core, z, xl, step):
    x = (xh * 2 + xl + step) % 4
    return (y, x // 2, core, z, x % 2)


X_OUT = pairs(lambda y, xh, c, z, xl: x_shift(y, xh, c, z, xl, 1 - 2 * c))
X_BACK = pairs(lambda y, xh, c, z, xl: x_shift(y, xh, c, z, xl, 2 * c - 1))
CORE = pairs(lambda y, xh, c, z, xl: (y, xh, 1 - c, z, xl))
Y_UP = [pairs(lambda y, xh, c, z, xl, d=d: (y + d, xh, c, z, xl)) for d in range(4)]
TURN = pairs(lambda y, xh, c, z, xl: (z // 2, xh, z % 2, y * 2 + c, xl))


def send(x, perm):
    return lax.ppermute(x, AXES, perm)


def rms_normed(rows):
    widened = rows.astype(jnp.float32)
    inv_rms = lax.rsqrt(jnp.mean(widened * widened, axis=-1, keepdims=True) + EPS)
    return (widened * inv_rms).astype(jnp.bfloat16)


def routing(counts, slot_of, slot_count):
    total_rows = slot_of.shape[0]
    numbers = jnp.arange(total_rows, dtype=jnp.int32)
    run_ends = jnp.cumsum(counts)
    starts = run_ends - counts
    sender = jnp.sum((run_ends[None, :] <= numbers[:, None]).astype(jnp.int32), axis=1)
    holder_ids = jnp.arange(counts.shape[0], dtype=jnp.int32)
    own_start = jnp.sum(
        jnp.where(sender[:, None] == holder_ids[None, :], starts[None, :], 0), axis=1
    )
    position = numbers - own_start
    owners = slot_of // slot_count
    within = slot_of % slot_count
    matches = (
        (sender[:, None] == sender[None, :])
        & (owners[:, None] == owners[None, :])
        & (numbers[None, :] < numbers[:, None])
    )
    ordinal = jnp.sum(matches.astype(jnp.int32), axis=1)
    return (sender, position, owners, within, ordinal)


def exchange(neighbours, counts, slot_of):
    seq = ("y", "xh", "core")
    seq_count = 16
    own_index = lax.axis_index(seq)
    tok_dev, capacity, feat = neighbours.shape
    pair_cap = -(-capacity // seq_count)
    slot_count = slot_of.shape[0] // seq_count
    columns = seq_count * pair_cap
    sender, position, owners, within, ordinal = routing(counts, slot_of, slot_count)
    send_col = owners * pair_cap + ordinal
    recv_col = sender * pair_cap + ordinal
    column_ids = jnp.arange(columns, dtype=jnp.int32)
    is_mine = sender == own_index
    pick_send = ((column_ids[:, None] == send_col[None, :]) & is_mine[None, :]).astype(jnp.bfloat16)
    pick_local = (jnp.arange(capacity, dtype=jnp.int32)[:, None] == position[None, :]).astype(
        jnp.bfloat16
    )
    select = jnp.dot(pick_send, pick_local.T, preferred_element_type=jnp.float32)
    is_ours = owners == own_index
    pick_slot = (
        (jnp.arange(slot_count, dtype=jnp.int32)[:, None] == within[None, :]) & is_ours[None, :]
    ).astype(jnp.bfloat16)
    pick_recv = (column_ids[:, None] == recv_col[None, :]).astype(jnp.bfloat16)
    placing = jnp.dot(pick_slot, pick_recv.T, preferred_element_type=jnp.float32)
    packed = jnp.einsum(
        "ki,tid->ktd", select.astype(jnp.bfloat16), neighbours, preferred_element_type=jnp.float32
    ).astype(jnp.bfloat16)
    packed = packed.reshape(columns * tok_dev, feat)
    arrived = lax.all_to_all(packed, seq, split_axis=0, concat_axis=0, tiled=True)
    placed = jnp.einsum(
        "jc,cr->jr",
        placing.astype(jnp.bfloat16),
        arrived.reshape(columns, tok_dev * feat),
        preferred_element_type=jnp.float32,
    ).astype(jnp.bfloat16)
    placed = placed.reshape(slot_count * tok_dev, feat)
    return lax.all_to_all(placed, ("z", "xl"), split_axis=0, concat_axis=0, tiled=True)


def body(
    hidden_states,
    query_weight,
    kv_weight,
    output_weight,
    enc_in_weight,
    enc_out_weight,
    neighbours,
    counts,
    slot_of,
):
    core = lax.axis_index("core")
    member = lax.axis_index(("y", "core"))
    feat = neighbours.shape[-1]

    half = enc_in_weight.shape[0] // 2
    in_half = lax.dynamic_slice_in_dim(enc_in_weight, core * half, half, 0)
    out_half = lax.dynamic_slice_in_dim(enc_out_weight, core * half, half, 0)
    in_mine = lax.all_gather(in_half, "z", axis=0, tiled=True)
    out_mine = lax.all_gather(out_half, "z", axis=0, tiled=True)
    in_rows = jnp.concatenate([in_mine, send(in_mine, CORE)], axis=0)
    out_rows = jnp.concatenate([out_mine, send(out_mine, CORE)], axis=0)

    def fetch(weight):
        rows = weight.shape[0] // 8
        piece = lax.dynamic_slice_in_dim(weight, member * rows, rows, 0)
        mine = lax.all_gather(send(piece, TURN), "z", axis=0, tiled=True)
        return mine, send(mine, X_OUT)

    kv_mine, kv_other = fetch(kv_weight.reshape(feat, -1))
    q_mine, q_other = fetch(query_weight)
    o_mine, o_other = fetch(output_weight)

    def spread(block):
        blocks = [block] + [send(block, Y_UP[d]) for d in (1, 2, 3)]
        own = jnp.concatenate(blocks, axis=0)
        return jnp.concatenate([own, send(own, CORE)], axis=0)

    tokens = spread(rms_normed(hidden_states))

    rows = exchange(neighbours, counts, slot_of)
    both = jnp.concatenate([rows, send(rows, X_OUT)], axis=0)
    hidden = lax.dot_general(
        rms_normed(both), in_rows, (((1,), (1,)), ((), ())), preferred_element_type=jnp.float32
    )
    hidden = jax.nn.gelu(hidden, approximate=False).astype(jnp.bfloat16)
    summed = jnp.dot(hidden, out_rows, preferred_element_type=jnp.float32)
    count = rows.shape[0]
    returned = send(summed[count:].astype(jnp.bfloat16), X_BACK)
    encoded = (
        rows.astype(jnp.float32) + summed[:count] + returned.astype(jnp.float32)
    ).astype(jnp.bfloat16)
    encoded = spread(encoded)

    spans = 8

    def attend(q_weight, kv_weight):
        queries = jnp.dot(tokens, q_weight, preferred_element_type=jnp.float32)
        queries = (queries * HD ** (-0.5)).astype(jnp.bfloat16)
        keyvals = jnp.dot(encoded, kv_weight, preferred_element_type=jnp.float32).astype(
            jnp.bfloat16
        )
        heads = q_weight.shape[1] // HD
        queries = queries.reshape(spans, CT, heads, HD)
        keyvals = keyvals.reshape(spans, count, 2, heads, HD)
        scores = jnp.einsum(
            "cqhe,ckhe->chqk", queries, keyvals[:, :, 0], preferred_element_type=jnp.float32
        )
        row_max = jnp.max(scores, axis=-1, keepdims=True)
        exponent = jnp.exp(scores - row_max)
        probs = (exponent / jnp.sum(exponent, axis=-1, keepdims=True)).astype(jnp.bfloat16)
        mixed = jnp.einsum(
            "chqk,ckhe->cqhe", probs, keyvals[:, :, 1], preferred_element_type=jnp.float32
        )
        return mixed.astype(jnp.bfloat16).reshape(spans * CT, heads * HD)

    mixed = jnp.concatenate([attend(q_mine, kv_mine), attend(q_other, kv_other)], axis=1)
    out_weight = jnp.concatenate([o_mine, o_other], axis=0)
    partial = jnp.dot(mixed, out_weight, preferred_element_type=jnp.float32)
    near, far = partial[: 4 * CT], partial[4 * CT :]
    near = near + send(far.astype(jnp.bfloat16), CORE).astype(jnp.float32)
    total = hidden_states.astype(jnp.float32) + near[:CT]
    for d in (1, 2, 3):
        block = near[d * CT : (d + 1) * CT].astype(jnp.bfloat16)
        total = total + send(block, Y_UP[4 - d]).astype(jnp.float32)
    return total.astype(jnp.bfloat16)


def solution(mesh):
    fine = Mesh(mesh.devices.reshape(SIZES), AXES)
    seq, blk = ("y", "xh", "core"), ("z", "xl")
    placed = (
        P(seq + blk, None),
        P(None, blk),
        P(None, None, blk),
        P(blk, None),
        P(blk, None),
        P(blk, None),
        P(blk, seq, None),
        P(),
        P(),
    )
    return jax.shard_map(
        body, mesh=fine, in_specs=placed, out_specs=P(seq + blk, None), check_vma=False
    )
```

```python
import jax
import jax.numpy as jnp
from jax import lax
from jax.experimental import pallas as pl
from jax.experimental.pallas import tpu as pltpu
from jax.sharding import Mesh, PartitionSpec as P

HD = 128
CT = 64
K_NB = 2
EPS = 1e-06
AXES = ("y", "xh", "core", "z", "xl")
SIZES = (4, 2, 2, 8, 2)


def coords_of(index):
    out = []
    for size in reversed(SIZES):
        out.append(index % size)
        index //= size
    return tuple(reversed(out))


def index_of(coords):
    index = 0
    for size, coord in zip(SIZES, coords):
        index = index * size + coord % size
    return index


def pairs(target):
    count = index_of(tuple(s - 1 for s in SIZES)) + 1
    return [(i, index_of(target(*coords_of(i)))) for i in range(count)]


def x_shift(y, xh, core, z, xl, step):
    x = (xh * 2 + xl + step) % 4
    return (y, x // 2, core, z, x % 2)


X_OUT = pairs(lambda y, xh, c, z, xl: x_shift(y, xh, c, z, xl, 1 - 2 * c))
X_BACK = pairs(lambda y, xh, c, z, xl: x_shift(y, xh, c, z, xl, 2 * c - 1))
CORE = pairs(lambda y, xh, c, z, xl: (y, xh, 1 - c, z, xl))
Y_UP = [pairs(lambda y, xh, c, z, xl, d=d: (y + d, xh, c, z, xl)) for d in range(4)]
Y_PAIR = pairs(lambda y, xh, c, z, xl: (y + 1 - 2 * c, xh, c, z, xl))
TURN = pairs(lambda y, xh, c, z, xl: (z // 2, xh, z % 2, y * 2 + c, xl))


def send(x, perm):
    return lax.ppermute(x, AXES, perm)


def rms_normed(rows):
    widened = rows.astype(jnp.float32)
    inv_rms = lax.rsqrt(jnp.mean(widened * widened, axis=-1, keepdims=True) + EPS)
    return (widened * inv_rms).astype(jnp.bfloat16)


def routing(counts, slot_of, slot_count):
    total_rows = slot_of.shape[0]
    numbers = jnp.arange(total_rows, dtype=jnp.int32)
    run_ends = jnp.cumsum(counts)
    starts = run_ends - counts
    sender = jnp.sum((run_ends[None, :] <= numbers[:, None]).astype(jnp.int32), axis=1)
    holder_ids = jnp.arange(counts.shape[0], dtype=jnp.int32)
    own_start = jnp.sum(
        jnp.where(sender[:, None] == holder_ids[None, :], starts[None, :], 0), axis=1
    )
    position = numbers - own_start
    owners = slot_of // slot_count
    within = slot_of % slot_count
    matches = (
        (sender[:, None] == sender[None, :])
        & (owners[:, None] == owners[None, :])
        & (numbers[None, :] < numbers[:, None])
    )
    ordinal = jnp.sum(matches.astype(jnp.int32), axis=1)
    return (sender, position, owners, within, ordinal)


def exchange(neighbours, counts, slot_of):
    seq = ("y", "xh", "core")
    seq_count = 16
    own_index = lax.axis_index(seq)
    tok_dev, capacity, feat = neighbours.shape
    pair_cap = -(-capacity // seq_count)
    slot_count = slot_of.shape[0] // seq_count
    columns = seq_count * pair_cap
    sender, position, owners, within, ordinal = routing(counts, slot_of, slot_count)
    send_col = owners * pair_cap + ordinal
    recv_col = sender * pair_cap + ordinal
    column_ids = jnp.arange(columns, dtype=jnp.int32)
    is_mine = sender == own_index
    pick_send = ((column_ids[:, None] == send_col[None, :]) & is_mine[None, :]).astype(jnp.bfloat16)
    pick_local = (jnp.arange(capacity, dtype=jnp.int32)[:, None] == position[None, :]).astype(
        jnp.bfloat16
    )
    select = jnp.dot(pick_send, pick_local.T, preferred_element_type=jnp.float32)
    is_ours = owners == own_index
    pick_slot = (
        (jnp.arange(slot_count, dtype=jnp.int32)[:, None] == within[None, :]) & is_ours[None, :]
    ).astype(jnp.bfloat16)
    pick_recv = (column_ids[:, None] == recv_col[None, :]).astype(jnp.bfloat16)
    placing = jnp.dot(pick_slot, pick_recv.T, preferred_element_type=jnp.float32)
    packed = jnp.einsum(
        "ki,tid->ktd", select.astype(jnp.bfloat16), neighbours, preferred_element_type=jnp.float32
    ).astype(jnp.bfloat16)
    packed = packed.reshape(columns * tok_dev, feat)
    arrived = lax.all_to_all(packed, seq, split_axis=0, concat_axis=0, tiled=True)
    placed = jnp.einsum(
        "jc,cr->jr",
        placing.astype(jnp.bfloat16),
        arrived.reshape(columns, tok_dev * feat),
        preferred_element_type=jnp.float32,
    ).astype(jnp.bfloat16)
    placed = placed.reshape(slot_count * tok_dev, feat)
    rows = lax.all_to_all(placed, ("z", "xl"), split_axis=0, concat_axis=0, tiled=True)
    return rows, packed, arrived


def matmul(a, b):
    return jnp.dot(a, b, preferred_element_type=jnp.float32)


def matmul_t(a, b):
    return lax.dot_general(a, b, (((1,), (1,)), ((), ())), preferred_element_type=jnp.float32)


def gelu(x):
    return 0.5 * x * (1.0 + lax.erf(x * (2.0**-0.5)))


def encode_kernel(steps, keep_raw, rows, in_a, in_b, out_a, out_b, result, normed, total):
    step = pl.program_id(0)

    @pl.when(step == 0)
    def _():
        normed[...] = rms_normed(rows[...])
        total[...] = jnp.zeros_like(total)

    for w_in, w_out in ((in_a, out_a), (in_b, out_b)):
        units = gelu(matmul_t(normed[...], w_in[...])).astype(jnp.bfloat16)
        total[...] += matmul(units, w_out[...])

    @pl.when(step == steps - 1)
    def _():
        summed = total[...]
        if keep_raw:
            summed = summed + rows[...].astype(jnp.float32)
        result[...] = summed.astype(result.dtype)


def encode(rows, in_a, in_b, out_a, out_b, keep_raw):
    count, feat = rows.shape
    units = in_a.shape[0]
    steps = 4
    weight = pl.BlockSpec((units // steps, feat), lambda i: (i, 0))
    whole = pl.BlockSpec((count, feat), lambda i: (0, 0))
    return pl.pallas_call(
        lambda *refs: encode_kernel(steps, keep_raw, *refs),
        grid=(steps,),
        in_specs=[whole, weight, weight, weight, weight],
        out_specs=whole,
        out_shape=jax.ShapeDtypeStruct((count, feat), jnp.float32 if keep_raw else jnp.bfloat16),
        scratch_shapes=[
            pltpu.VMEM((count, feat), jnp.bfloat16),
            pltpu.VMEM((count, feat), jnp.float32),
        ],
        compiler_params=pltpu.CompilerParams(vmem_limit_bytes=32 * 2**20),
        cost_estimate=pl.CostEstimate(
            flops=8 * count * units * feat,
            bytes_accessed=8 * units * feat + 6 * count * feat,
            transcendentals=2 * count * units,
        ),
        name="encode",
    )(rows, in_a, in_b, out_a, out_b)


def attend_kernel(first, q_a, q_b, enc_0, enc_1, k_a, v_a, k_b, v_b, mixed):
    for span, enc in enumerate((enc_0, enc_1)):
        source = enc[...]
        row = first + span * 4 * CT
        for half, (q, k, v) in enumerate(((q_a, k_a, v_a), (q_b, k_b, v_b))):
            keys = matmul(source, k[...]).astype(jnp.bfloat16)
            values = matmul(source, v[...]).astype(jnp.bfloat16)
            for head in range(2):
                columns = slice(head * HD, (head + 1) * HD)
                scores = matmul_t(q[row : row + CT, columns], keys[:, columns])
                exponent = jnp.exp(scores - jnp.max(scores, axis=-1, keepdims=True))
                probs = exponent / jnp.sum(exponent, axis=-1, keepdims=True)
                out = matmul(probs.astype(jnp.bfloat16), values[:, columns])
                start = half * 2 * HD + head * HD
                mixed[span * CT : (span + 1) * CT, start : start + HD] = out.astype(jnp.bfloat16)


def attend(first, *args):
    enc = args[2]
    return pl.pallas_call(
        lambda *refs: attend_kernel(first, *refs),
        out_shape=jax.ShapeDtypeStruct((2 * CT, 4 * HD), jnp.bfloat16),
        compiler_params=pltpu.CompilerParams(vmem_limit_bytes=32 * 2**20),
        cost_estimate=pl.CostEstimate(
            flops=2 * 2 * enc.shape[0] * enc.shape[1] * 8 * HD,
            bytes_accessed=2 * sum(arg.size for arg in args),
            transcendentals=8 * CT * enc.shape[0],
        ),
        name="attend",
    )(*args)


def project_kernel(mixed, o_a, o_b, near, far):
    rows = mixed[...]
    half = o_a.shape[0]
    out = matmul(rows[:, :half], o_a[...]) + matmul(rows[:, half:], o_b[...])
    near[...] = out[:CT]
    far[...] = out[CT:].astype(jnp.bfloat16)


def project(mixed, o_a, o_b):
    depth, width = o_a.shape
    block = 1024
    weight = pl.BlockSpec((depth, block), lambda i: (0, i))
    out = pl.BlockSpec((CT, block), lambda i: (0, i))
    return pl.pallas_call(
        project_kernel,
        grid=(width // block,),
        in_specs=[pl.BlockSpec(mixed.shape, lambda i: (0, 0)), weight, weight],
        out_specs=[out, out],
        out_shape=[
            jax.ShapeDtypeStruct((CT, width), jnp.float32),
            jax.ShapeDtypeStruct((CT, width), jnp.bfloat16),
        ],
        compiler_params=pltpu.CompilerParams(vmem_limit_bytes=32 * 2**20),
        cost_estimate=pl.CostEstimate(
            flops=4 * mixed.shape[0] * depth * width,
            bytes_accessed=4 * depth * width + 6 * CT * width,
            transcendentals=0,
        ),
        name="project",
    )(mixed, o_a, o_b)


def after(value, earlier):
    return lax.optimization_barrier((value, earlier))[0]


def body(
    hidden_states,
    query_weight,
    kv_weight,
    output_weight,
    enc_in_weight,
    enc_out_weight,
    neighbours,
    counts,
    slot_of,
):
    core = lax.axis_index("core")
    odd_y = lax.axis_index("y") % 2
    member = lax.axis_index(("y", "core"))
    feat = neighbours.shape[-1]

    half = enc_in_weight.shape[0] // 2
    both_sides = jnp.where(odd_y == 0, enc_in_weight, enc_out_weight)
    mine = lax.all_gather(
        lax.dynamic_slice_in_dim(both_sides, core * half, half, 0), "z", axis=0, tiled=True
    )
    paired = send(mine, Y_PAIR)
    mine = (mine, send(mine, CORE))
    paired = (paired, send(paired, CORE))
    enc_in = [jnp.where(odd_y == 0, a, b) for a, b in zip(mine, paired)]
    enc_out = [jnp.where(odd_y == 0, b, a) for a, b in zip(mine, paired)]

    rows, packed, arrived = exchange(neighbours, counts, slot_of)

    def piece_of(weight):
        count = weight.shape[0] // 8
        return lax.dynamic_slice_in_dim(weight, member * count, count, 0)

    kv_piece = piece_of(kv_weight)
    in_piece = jnp.concatenate([piece_of(query_weight), kv_piece[:, 0], kv_piece[:, 1]], axis=0)
    out_piece = piece_of(output_weight)
    in_piece, out_piece = send(after(in_piece, packed), TURN), send(after(out_piece, packed), TURN)
    gathered_in = lax.all_gather(in_piece, "z", axis=0, tiled=True)
    out_a = lax.all_gather(out_piece, "z", axis=0, tiled=True)

    def unpack(gathered):
        parts = gathered.reshape(8, -1, gathered.shape[1])
        rows_q, rows_k = query_weight.shape[0] // 8, feat // 8
        cuts = (0, rows_q, rows_q + rows_k, rows_q + 2 * rows_k)
        return [
            parts[:, a:b].reshape(8 * (b - a), -1) for a, b in zip(cuts[:-1], cuts[1:])
        ]

    qw_a, kw_a, vw_a = unpack(gathered_in)
    qw_b, kw_b, vw_b = unpack(send(gathered_in, X_OUT))
    out_b = send(out_a, X_OUT)

    normed = after(rms_normed(hidden_states), arrived)
    tokens = jnp.concatenate([normed] + [send(normed, Y_UP[d]) for d in (1, 2, 3)], axis=0)
    tokens = jnp.concatenate([tokens, send(tokens, CORE)], axis=0)

    def query(weight):
        return (matmul(tokens, weight) * HD ** (-0.5)).astype(jnp.bfloat16)

    queries = query(qw_a), query(qw_b)

    weights = enc_in + enc_out
    visitors = send(rows, X_OUT)
    returned = send(encode(visitors, *weights, keep_raw=False), X_BACK)
    encoded = encode(rows, *weights, keep_raw=True)
    encoded = (encoded + returned.astype(jnp.float32)).astype(jnp.bfloat16)
    blocks = [encoded] + [send(encoded, Y_UP[d]) for d in (1, 2, 3)]

    total = hidden_states.astype(jnp.float32)
    for d in (2, 1, 3, 0):
        mixed = attend(
            d * CT, *queries, blocks[d], send(blocks[d], CORE), kw_a, vw_a, kw_b, vw_b
        )
        near, far = project(mixed, out_a, out_b)
        near = near + send(far, CORE).astype(jnp.float32)
        if d:
            near = send(near.astype(jnp.bfloat16), Y_UP[4 - d]).astype(jnp.float32)
        total = total + near
    return total.astype(jnp.bfloat16)


def solution(mesh):
    fine = Mesh(mesh.devices.reshape(SIZES), AXES)
    seq, blk = ("y", "xh", "core"), ("z", "xl")
    placed = (
        P(seq + blk, None),
        P(None, blk),
        P(None, None, blk),
        P(blk, None),
        P(blk, None),
        P(blk, None),
        P(blk, seq, None),
        P(),
        P(),
    )
    return jax.shard_map(
        body, mesh=fine, in_specs=placed, out_specs=P(seq + blk, None), check_vma=False
    )
```

```python
import jax
import jax.numpy as jnp
from jax import lax
from jax.experimental import pallas as pl
from jax.experimental.pallas import tpu as pltpu
from jax.sharding import Mesh, PartitionSpec as P

HD = 128
CT = 64
K_NB = 2
EPS = 1e-06
AXES = ("y", "xh", "core", "z", "xl")
SIZES = (4, 2, 2, 8, 2)


def coords_of(index):
    out = []
    for size in reversed(SIZES):
        out.append(index % size)
        index //= size
    return tuple(reversed(out))


def index_of(coords):
    index = 0
    for size, coord in zip(SIZES, coords):
        index = index * size + coord % size
    return index


def pairs(target):
    count = index_of(tuple(s - 1 for s in SIZES)) + 1
    return [(i, index_of(target(*coords_of(i)))) for i in range(count)]


def x_shift(y, xh, core, z, xl, step):
    x = (xh * 2 + xl + step) % 4
    return (y, x // 2, core, z, x % 2)


X_OUT = pairs(lambda y, xh, c, z, xl: x_shift(y, xh, c, z, xl, 1 - 2 * c))
X_BACK = pairs(lambda y, xh, c, z, xl: x_shift(y, xh, c, z, xl, 2 * c - 1))
CORE = pairs(lambda y, xh, c, z, xl: (y, xh, 1 - c, z, xl))
Y_UP = [pairs(lambda y, xh, c, z, xl, d=d: (y + d, xh, c, z, xl)) for d in range(4)]
Y_PAIR = pairs(lambda y, xh, c, z, xl: (y + 1 - 2 * c, xh, c, z, xl))


Z_UP = pairs(lambda y, xh, c, z, xl: (y, xh, c, z + 1, xl))
Z_DOWN = pairs(lambda y, xh, c, z, xl: (y, xh, c, z - 1, xl))
RING = (0, -1, 1, -2, 2, -3, 3, -4)
def steps_a(y, core):
    return (y, 4 if y == 0 else 8 - y)[core]


def steps_b(y, core):
    return ((4 - y) % 4, y + 4)[core]


def along_z(steps):
    return pairs(lambda y, xh, c, z, xl: (y, xh, c, z + steps(y, c), xl))


def to_member(steps):
    def target(y, xh, c, z, xl):
        member = (z - steps(y, c)) % 8
        return (member // 2, xh, member % 2, z, xl)

    return pairs(target)


def own_steps(steps):
    table = [steps(m // 2, m % 2) for m in range(8)]
    member = lax.axis_index(("y", "core"))
    return sum(jnp.where(member == m, d, 0) for m, d in enumerate(table))


def send(x, perm):
    return lax.ppermute(x, AXES, perm)


def rms_normed(rows):
    widened = rows.astype(jnp.float32)
    inv_rms = lax.rsqrt(jnp.mean(widened * widened, axis=-1, keepdims=True) + EPS)
    return (widened * inv_rms).astype(jnp.bfloat16)


def routing(counts, slot_of, slot_count):
    total_rows = slot_of.shape[0]
    numbers = jnp.arange(total_rows, dtype=jnp.int32)
    run_ends = jnp.cumsum(counts)
    starts = run_ends - counts
    sender = jnp.sum((run_ends[None, :] <= numbers[:, None]).astype(jnp.int32), axis=1)
    holder_ids = jnp.arange(counts.shape[0], dtype=jnp.int32)
    own_start = jnp.sum(
        jnp.where(sender[:, None] == holder_ids[None, :], starts[None, :], 0), axis=1
    )
    position = numbers - own_start
    owners = slot_of // slot_count
    within = slot_of % slot_count
    matches = (
        (sender[:, None] == sender[None, :])
        & (owners[:, None] == owners[None, :])
        & (numbers[None, :] < numbers[:, None])
    )
    ordinal = jnp.sum(matches.astype(jnp.int32), axis=1)
    return (sender, position, owners, within, ordinal)


def pack(neighbours, counts, slot_of):
    seq = ("y", "xh", "core")
    seq_count = 16
    own_index = lax.axis_index(seq)
    tok_dev, capacity, feat = neighbours.shape
    pair_cap = -(-capacity // seq_count)
    slot_count = slot_of.shape[0] // seq_count
    columns = seq_count * pair_cap
    sender, position, owners, within, ordinal = routing(counts, slot_of, slot_count)
    send_col = owners * pair_cap + ordinal
    recv_col = sender * pair_cap + ordinal
    column_ids = jnp.arange(columns, dtype=jnp.int32)
    is_mine = sender == own_index
    pick_send = ((column_ids[:, None] == send_col[None, :]) & is_mine[None, :]).astype(jnp.bfloat16)
    pick_local = (jnp.arange(capacity, dtype=jnp.int32)[:, None] == position[None, :]).astype(
        jnp.bfloat16
    )
    select = jnp.dot(pick_send, pick_local.T, preferred_element_type=jnp.float32)
    is_ours = owners == own_index
    pick_slot = (
        (jnp.arange(slot_count, dtype=jnp.int32)[:, None] == within[None, :]) & is_ours[None, :]
    ).astype(jnp.bfloat16)
    pick_recv = (column_ids[:, None] == recv_col[None, :]).astype(jnp.bfloat16)
    placing = jnp.dot(pick_slot, pick_recv.T, preferred_element_type=jnp.float32)
    packed = jnp.einsum(
        "ki,tid->ktd", select.astype(jnp.bfloat16), neighbours, preferred_element_type=jnp.float32
    ).astype(jnp.bfloat16)
    return packed.reshape(columns * tok_dev, feat), placing.astype(jnp.bfloat16)


def place(arrived, placing):
    slot_count, columns = placing.shape
    placed = jnp.einsum(
        "jc,cr->jr", placing, arrived.reshape(columns, -1), preferred_element_type=jnp.float32
    )
    return placed.astype(jnp.bfloat16).reshape(-1, arrived.shape[1])


def matmul(a, b):
    return jnp.dot(a, b, preferred_element_type=jnp.float32)


def matmul_t(a, b):
    return lax.dot_general(a, b, (((1,), (1,)), ((), ())), preferred_element_type=jnp.float32)


def gelu(x):
    return 0.5 * x * (1.0 + lax.erf(x * (2.0**-0.5)))


def encode_kernel(steps, keep_raw, rows, in_a, in_b, out_a, out_b, result, normed, total):
    step = pl.program_id(0)

    @pl.when(step == 0)
    def _():
        normed[...] = rms_normed(rows[...])
        total[...] = jnp.zeros_like(total)

    for w_in, w_out in ((in_a, out_a), (in_b, out_b)):
        units = gelu(matmul_t(normed[...], w_in[...])).astype(jnp.bfloat16)
        total[...] += matmul(units, w_out[...])

    @pl.when(step == steps - 1)
    def _():
        summed = total[...]
        if keep_raw:
            summed = summed + rows[...].astype(jnp.float32)
        result[...] = summed.astype(result.dtype)


def encode(rows, in_a, in_b, out_a, out_b, keep_raw):
    count, feat = rows.shape
    units = in_a.shape[0]
    steps = 4
    weight = pl.BlockSpec((units // steps, feat), lambda i: (i, 0))
    whole = pl.BlockSpec((count, feat), lambda i: (0, 0))
    return pl.pallas_call(
        lambda *refs: encode_kernel(steps, keep_raw, *refs),
        grid=(steps,),
        in_specs=[whole, weight, weight, weight, weight],
        out_specs=whole,
        out_shape=jax.ShapeDtypeStruct((count, feat), jnp.float32 if keep_raw else jnp.bfloat16),
        scratch_shapes=[
            pltpu.VMEM((count, feat), jnp.bfloat16),
            pltpu.VMEM((count, feat), jnp.float32),
        ],
        compiler_params=pltpu.CompilerParams(vmem_limit_bytes=32 * 2**20),
        cost_estimate=pl.CostEstimate(flops=1, bytes_accessed=1, transcendentals=0),
        name="encode",
    )(rows, in_a, in_b, out_a, out_b)


def query_kernel(tokens, *refs):
    total, start = 0.0, 0
    for weight in refs[:-1]:
        depth = weight.shape[0]
        total = total + matmul(tokens[:, start : start + depth], weight[...])
        start += depth
    refs[-1][...] = (total * HD ** (-0.5)).astype(jnp.bfloat16)


def query(tokens, weights):
    return pl.pallas_call(
        query_kernel,
        out_shape=jax.ShapeDtypeStruct((tokens.shape[0], weights[0].shape[1]), jnp.bfloat16),
        compiler_params=pltpu.CompilerParams(vmem_limit_bytes=40 * 2**20),
        cost_estimate=pl.CostEstimate(flops=1, bytes_accessed=1, transcendentals=0),
        name="query",
    )(tokens, *weights)


def attend_kernel(first, q, enc_0, enc_1, kv, mixed):
    feat = kv.shape[0] // 2
    for span, enc in enumerate((enc_0, enc_1)):
        source = enc[...]
        row = first + span * 4 * CT
        keys = matmul(source, kv[:feat]).astype(jnp.bfloat16)
        values = matmul(source, kv[feat:]).astype(jnp.bfloat16)
        for head in range(2):
            columns = slice(head * HD, (head + 1) * HD)
            scores = matmul_t(q[row : row + CT, columns], keys[:, columns])
            exponent = jnp.exp(scores - jnp.max(scores, axis=-1, keepdims=True))
            probs = exponent / jnp.sum(exponent, axis=-1, keepdims=True)
            out = matmul(probs.astype(jnp.bfloat16), values[:, columns])
            mixed[span * CT : (span + 1) * CT, columns] = out.astype(jnp.bfloat16)


def attend(first, q, enc_0, enc_1, kv):
    return pl.pallas_call(
        lambda *refs: attend_kernel(first, *refs),
        out_shape=jax.ShapeDtypeStruct((2 * CT, q.shape[1]), jnp.bfloat16),
        compiler_params=pltpu.CompilerParams(vmem_limit_bytes=32 * 2**20),
        cost_estimate=pl.CostEstimate(flops=1, bytes_accessed=1, transcendentals=0),
        name="attend",
    )(q, enc_0, enc_1, kv)


def project_kernel(mixed_a, mixed_b, o_a, o_b, near, far):
    half = mixed_a.shape[1]
    width = o_a.shape[1]
    for block in range(o_a.shape[0] // half):
        depth = slice(block * half, (block + 1) * half)
        columns = slice(block * width, (block + 1) * width)
        out = matmul(mixed_a[...], o_a[depth]) + matmul(mixed_b[...], o_b[depth])
        near[:, columns] = out[:CT]
        far[:, columns] = out[CT:].astype(jnp.bfloat16)


def project(mixed_a, mixed_b, o_a, o_b):
    count, half = mixed_a.shape
    blocks = o_a.shape[0] // half
    step = blocks // 4
    width = blocks * o_a.shape[1]
    rows = pl.BlockSpec((count, half), lambda i: (0, 0))
    weight = pl.BlockSpec((step * half, o_a.shape[1]), lambda i: (i, 0))
    out = pl.BlockSpec((CT, step * o_a.shape[1]), lambda i: (0, i))
    return pl.pallas_call(
        project_kernel,
        grid=(4,),
        in_specs=[rows, rows, weight, weight],
        out_specs=[out, out],
        out_shape=[
            jax.ShapeDtypeStruct((CT, width), jnp.float32),
            jax.ShapeDtypeStruct((CT, width), jnp.bfloat16),
        ],
        compiler_params=pltpu.CompilerParams(vmem_limit_bytes=32 * 2**20),
        cost_estimate=pl.CostEstimate(flops=1, bytes_accessed=1, transcendentals=0),
        name="project",
    )(mixed_a, mixed_b, o_a, o_b)


def after(value, *earlier):
    return lax.optimization_barrier((value, *earlier))[0]


def together(*values):
    return lax.optimization_barrier(values)


def body(
    hidden_states,
    query_weight,
    kv_weight,
    output_weight,
    enc_in_weight,
    enc_out_weight,
    neighbours,
    counts,
    slot_of,
):
    core = lax.axis_index("core")
    plane = lax.axis_index("z")
    odd_y = lax.axis_index("y") % 2
    feat = neighbours.shape[-1]

    half = enc_in_weight.shape[0] // 2
    side = jnp.where(odd_y == 0, enc_in_weight, enc_out_weight)
    mine = lax.all_gather(
        lax.dynamic_slice_in_dim(side, core * half, half, 0), "z", axis=0, tiled=True
    )

    def piece_of(weight, steps, axis):
        count = weight.shape[axis] // 8
        index = (plane + own_steps(steps)) % 8
        return lax.dynamic_slice_in_dim(weight, index * count, count, axis)

    width = query_weight.shape[1]
    q_piece = piece_of(query_weight, steps_a, 0)
    kv_piece = piece_of(kv_weight, steps_b, 0)
    o_piece = piece_of(output_weight, steps_b, 1)
    o_piece = [o_piece[:, i : i + width] for i in range(0, o_piece.shape[1], width)]
    kvo_piece = jnp.concatenate([kv_piece[:, 0], kv_piece[:, 1]] + o_piece, axis=0)

    normed = rms_normed(hidden_states)
    columns = normed.shape[1] // 8
    normed = jnp.concatenate(
        [
            lax.dynamic_slice_in_dim(normed, (plane + 8 + d) % 8 * columns, columns, 1)
            for d in RING
        ],
        axis=1,
    )

    packed, placing = pack(neighbours, counts, slot_of)
    arrived = lax.all_to_all(packed, ("y", "xh", "core"), split_axis=0, concat_axis=0, tiled=True)
    q_piece, kvo_piece, packed = together(q_piece, kvo_piece, packed)
    q_piece = send(q_piece, along_z(steps_a))
    kvo_piece = send(kvo_piece, along_z(steps_b))
    normed = after(normed, packed)
    tokens = {0: normed, 1: send(normed, Y_UP[1]), 3: send(normed, Y_UP[3])}
    placed = place(arrived, placing)

    placed, q_piece, kvo_piece, tokens[1], tokens[3] = together(
        placed, q_piece, kvo_piece, tokens[1], tokens[3]
    )
    rows = lax.all_to_all(placed, ("z", "xl"), split_axis=0, concat_axis=0, tiled=True)
    q_piece = send(q_piece, to_member(steps_a))
    kvo_piece = send(kvo_piece, to_member(steps_b))

    rows, q_piece, kvo_piece, mine = together(rows, q_piece, kvo_piece, mine)
    gathered = lax.all_gather(kvo_piece, "z", axis=0, tiled=True)
    paired = send(mine, Y_PAIR)
    mine = [mine, send(mine, CORE)]
    visitors = send(rows, X_OUT)
    up, down = send(q_piece, Z_UP), send(q_piece, Z_DOWN)

    paired, visitors, mine[1] = together(paired, visitors, mine[1])
    paired = [paired, send(paired, CORE)]
    tokens[2] = send(after(normed, visitors), Y_UP[2])

    up, down, paired[1] = together(up, down, paired[1])
    enc_in = [jnp.where(odd_y == 0, a, b) for a, b in zip(mine, paired)]
    enc_out = [jnp.where(odd_y == 0, b, a) for a, b in zip(mine, paired)]
    q_a = [jnp.concatenate([q_piece, up, down], axis=0)]
    up, down = send(up, Z_UP), send(down, Z_DOWN)
    q_b = [send(q_a[0], X_OUT)]
    visited = encode(visitors, *enc_in, *enc_out, keep_raw=False)

    up, down, visited = together(up, down, visited)
    returned = send(visited, X_BACK)
    q_a.append(jnp.concatenate([up, down], axis=0))
    up, down = send(up, Z_UP), send(down, Z_DOWN)
    q_b.append(send(q_a[1], X_OUT))
    parts = after(gathered, visited).reshape(8, -1, width)
    k_rows = feat // 8
    kv_a = jnp.concatenate(
        [parts[:, :k_rows].reshape(feat, width), parts[:, k_rows : 2 * k_rows].reshape(feat, width)],
        axis=0,
    )
    o_a = parts[:, 2 * k_rows :].reshape(-1, width)
    kv_b, o_b = send(kv_a, X_OUT), send(o_a, X_OUT)
    encoded = encode(after(rows, visited), *enc_in, *enc_out, keep_raw=True)
    encoded = (encoded + returned.astype(jnp.float32)).astype(jnp.bfloat16)

    encoded, up, down = together(encoded, up, down)
    blocks = [encoded] + [send(encoded, Y_UP[d]) for d in (1, 2, 3)]
    q_a.append(jnp.concatenate([up, down], axis=0))
    q_b.append(send(q_a[2], X_OUT))
    q_a.append(send(up, Z_UP))
    q_b.append(send(q_a[3], X_OUT))

    tokens = jnp.concatenate([tokens[d] for d in range(4)], axis=0)
    tokens = jnp.concatenate([tokens, send(tokens, CORE)], axis=0)
    others = [send(block, CORE) for block in blocks]
    queries = query(tokens, q_a), query(tokens, q_b)

    total = hidden_states.astype(jnp.float32)
    for d in (2, 1, 3, 0):
        mixed_a = attend(d * CT, queries[0], blocks[d], others[d], kv_a)
        mixed_b = attend(d * CT, queries[1], blocks[d], others[d], kv_b)
        near, far = project(mixed_a, mixed_b, o_a, o_b)
        kv_a, kv_b, near, far = together(kv_a, kv_b, near, far)
        near = near + send(far, CORE).astype(jnp.float32)
        if d:
            near = send(near.astype(jnp.bfloat16), Y_UP[4 - d]).astype(jnp.float32)
        total = total + near
    return total.astype(jnp.bfloat16)


def solution(mesh):
    fine = Mesh(mesh.devices.reshape(SIZES), AXES)
    seq, blk = ("y", "xh", "core"), ("z", "xl")
    placed = (
        P(seq + blk, None),
        P(None, blk),
        P(None, None, blk),
        P(blk, None),
        P(blk, None),
        P(blk, None),
        P(blk, seq, None),
        P(),
        P(),
    )
    return jax.shard_map(
        body, mesh=fine, in_specs=placed, out_specs=P(seq + blk, None), check_vma=False
    )
```

```python
import jax
import jax.numpy as jnp
from jax import lax
from jax.experimental import pallas as pl
from jax.experimental.pallas import tpu as pltpu
from jax.sharding import Mesh, PartitionSpec as P

HD = 128
CT = 64
K_NB = 2
EPS = 1e-06
AXES = ("y", "xh", "core", "z", "xl")
SIZES = (4, 2, 2, 8, 2)


def coords_of(index):
    out = []
    for size in reversed(SIZES):
        out.append(index % size)
        index //= size
    return tuple(reversed(out))


def index_of(coords):
    index = 0
    for size, coord in zip(SIZES, coords):
        index = index * size + coord % size
    return index


def pairs(target):
    count = index_of(tuple(s - 1 for s in SIZES)) + 1
    return [(i, index_of(target(*coords_of(i)))) for i in range(count)]


def x_shift(y, xh, core, z, xl, step):
    x = (xh * 2 + xl + step) % 4
    return (y, x // 2, core, z, x % 2)


X_OUT = pairs(lambda y, xh, c, z, xl: x_shift(y, xh, c, z, xl, 1 - 2 * c))
X_BACK = pairs(lambda y, xh, c, z, xl: x_shift(y, xh, c, z, xl, 2 * c - 1))
CORE = pairs(lambda y, xh, c, z, xl: (y, xh, 1 - c, z, xl))
Y_UP = [pairs(lambda y, xh, c, z, xl, d=d: (y + d, xh, c, z, xl)) for d in range(4)]
def steps_a(y, core):
    return (y, 4 if y == 0 else 8 - y)[core]


def steps_b(y, core):
    return ((4 - y) % 4, y + 4)[core]


def along_z(steps):
    return pairs(lambda y, xh, c, z, xl: (y, xh, c, z + steps(y, c), xl))


def to_member(steps):
    def target(y, xh, c, z, xl):
        member = (z - steps(y, c)) % 8
        return (member // 2, xh, member % 2, z, xl)

    return pairs(target)


def own_steps(steps):
    table = [steps(m // 2, m % 2) for m in range(8)]
    member = lax.axis_index(("y", "core"))
    return sum(jnp.where(member == m, d, 0) for m, d in enumerate(table))


def send(x, perm):
    return lax.ppermute(x, AXES, perm)


def rms_normed(rows):
    widened = rows.astype(jnp.float32)
    inv_rms = lax.rsqrt(jnp.mean(widened * widened, axis=-1, keepdims=True) + EPS)
    return (widened * inv_rms).astype(jnp.bfloat16)


def routing(counts, slot_of, slot_count):
    total_rows = slot_of.shape[0]
    numbers = jnp.arange(total_rows, dtype=jnp.int32)
    run_ends = jnp.cumsum(counts)
    starts = run_ends - counts
    sender = jnp.sum((run_ends[None, :] <= numbers[:, None]).astype(jnp.int32), axis=1)
    holder_ids = jnp.arange(counts.shape[0], dtype=jnp.int32)
    own_start = jnp.sum(
        jnp.where(sender[:, None] == holder_ids[None, :], starts[None, :], 0), axis=1
    )
    position = numbers - own_start
    owners = slot_of // slot_count
    within = slot_of % slot_count
    matches = (
        (sender[:, None] == sender[None, :])
        & (owners[:, None] == owners[None, :])
        & (numbers[None, :] < numbers[:, None])
    )
    ordinal = jnp.sum(matches.astype(jnp.int32), axis=1)
    return (sender, position, owners, within, ordinal)


def pack(neighbours, counts, slot_of):
    seq = ("y", "xh", "core")
    seq_count = 16
    own_index = lax.axis_index(seq)
    tok_dev, capacity, feat = neighbours.shape
    pair_cap = -(-capacity // seq_count)
    slot_count = slot_of.shape[0] // seq_count
    columns = seq_count * pair_cap
    sender, position, owners, within, ordinal = routing(counts, slot_of, slot_count)
    send_col = owners * pair_cap + ordinal
    recv_col = sender * pair_cap + ordinal
    column_ids = jnp.arange(columns, dtype=jnp.int32)
    is_mine = sender == own_index
    pick_send = ((column_ids[:, None] == send_col[None, :]) & is_mine[None, :]).astype(jnp.bfloat16)
    pick_local = (jnp.arange(capacity, dtype=jnp.int32)[:, None] == position[None, :]).astype(
        jnp.bfloat16
    )
    select = jnp.dot(pick_send, pick_local.T, preferred_element_type=jnp.float32)
    is_ours = owners == own_index
    pick_slot = (
        (jnp.arange(slot_count, dtype=jnp.int32)[:, None] == within[None, :]) & is_ours[None, :]
    ).astype(jnp.bfloat16)
    pick_recv = (column_ids[:, None] == recv_col[None, :]).astype(jnp.bfloat16)
    placing = jnp.dot(pick_slot, pick_recv.T, preferred_element_type=jnp.float32)
    packed = jnp.einsum(
        "ki,tid->ktd", select.astype(jnp.bfloat16), neighbours, preferred_element_type=jnp.float32
    ).astype(jnp.bfloat16)
    return packed.reshape(columns * tok_dev, feat), placing.astype(jnp.bfloat16)


def place(arrived, placing):
    slot_count, columns = placing.shape
    placed = jnp.einsum(
        "jc,cr->jr", placing, arrived.reshape(columns, -1), preferred_element_type=jnp.float32
    )
    return placed.astype(jnp.bfloat16).reshape(-1, arrived.shape[1])


def matmul(a, b):
    return jnp.dot(a, b, preferred_element_type=jnp.float32)


def matmul_t(a, b):
    return lax.dot_general(a, b, (((1,), (1,)), ((), ())), preferred_element_type=jnp.float32)


def gelu(x):
    return 0.5 * x * (1.0 + lax.erf(x * (2.0**-0.5)))


def encode_kernel(steps, keep_raw, rows, mine, other, result, normed, total):
    step = pl.program_id(0)

    @pl.when(step == 0)
    def _():
        normed[...] = rms_normed(rows[...])
        total[...] = jnp.zeros_like(total)

    for block in (mine, other):
        parts = [block[i] for i in range(block.shape[0])]
        w_in, w_out = jnp.concatenate(parts[0::2], axis=0), jnp.concatenate(parts[1::2], axis=0)
        units = gelu(matmul_t(normed[...], w_in)).astype(jnp.bfloat16)
        total[...] += matmul(units, w_out)

    @pl.when(step == steps - 1)
    def _():
        summed = total[...]
        if keep_raw:
            summed = summed + rows[...].astype(jnp.float32)
        result[...] = summed.astype(result.dtype)


def encode(rows, mine, other, keep_raw):
    count, feat = rows.shape
    planes = 8
    steps = 4
    mine, other = (w.reshape(2 * planes, -1, feat) for w in (mine, other))
    weight = pl.BlockSpec((2 * planes // steps,) + mine.shape[1:], lambda i: (i, 0, 0))
    whole = pl.BlockSpec((count, feat), lambda i: (0, 0))
    return pl.pallas_call(
        lambda *refs: encode_kernel(steps, keep_raw, *refs),
        grid=(steps,),
        in_specs=[whole, weight, weight],
        out_specs=whole,
        out_shape=jax.ShapeDtypeStruct((count, feat), jnp.float32 if keep_raw else jnp.bfloat16),
        scratch_shapes=[
            pltpu.VMEM((count, feat), jnp.bfloat16),
            pltpu.VMEM((count, feat), jnp.float32),
        ],
        compiler_params=pltpu.CompilerParams(vmem_limit_bytes=32 * 2**20),
        cost_estimate=pl.CostEstimate(flops=1, bytes_accessed=1, transcendentals=0),
        name="encode",
    )(rows, mine, other)


def query_kernel(tokens, weight, result):
    projected = matmul(tokens[...], weight[...])
    result[...] = (projected * HD ** (-0.5)).astype(jnp.bfloat16)


def query(tokens, weight):
    return pl.pallas_call(
        query_kernel,
        out_shape=jax.ShapeDtypeStruct((tokens.shape[0], weight.shape[1]), jnp.bfloat16),
        compiler_params=pltpu.CompilerParams(vmem_limit_bytes=40 * 2**20),
        cost_estimate=pl.CostEstimate(flops=1, bytes_accessed=1, transcendentals=0),
        name="query",
    )(tokens, weight)


def attend_kernel(first, q, enc_0, enc_1, kv, mixed):
    feat = kv.shape[0] // 2
    for span, enc in enumerate((enc_0, enc_1)):
        source = enc[...]
        row = first + span * 4 * CT
        keys = matmul(source, kv[:feat]).astype(jnp.bfloat16)
        values = matmul(source, kv[feat:]).astype(jnp.bfloat16)
        for head in range(2):
            columns = slice(head * HD, (head + 1) * HD)
            scores = matmul_t(q[row : row + CT, columns], keys[:, columns])
            exponent = jnp.exp(scores - jnp.max(scores, axis=-1, keepdims=True))
            probs = exponent / jnp.sum(exponent, axis=-1, keepdims=True)
            out = matmul(probs.astype(jnp.bfloat16), values[:, columns])
            mixed[span * CT : (span + 1) * CT, columns] = out.astype(jnp.bfloat16)


def attend(first, q, enc_0, enc_1, kv):
    return pl.pallas_call(
        lambda *refs: attend_kernel(first, *refs),
        out_shape=jax.ShapeDtypeStruct((2 * CT, q.shape[1]), jnp.bfloat16),
        compiler_params=pltpu.CompilerParams(vmem_limit_bytes=32 * 2**20),
        cost_estimate=pl.CostEstimate(flops=1, bytes_accessed=1, transcendentals=0),
        name="attend",
    )(q, enc_0, enc_1, kv)


def project_kernel(mixed_a, mixed_b, weight, near, far):
    half = mixed_a.shape[1]
    width = weight.shape[3]
    for plane in range(weight.shape[0]):
        for block in range(weight.shape[1] // 2):
            start = (plane * weight.shape[1] // 2 + block) * width
            out = matmul(mixed_a[...], weight[plane, block])
            out = out + matmul(mixed_b[...], weight[plane, weight.shape[1] // 2 + block])
            near[:, start : start + width] = out[:CT]
            far[:, start : start + width] = out[CT:].astype(jnp.bfloat16)


def project(mixed_a, mixed_b, weight):
    count, half = mixed_a.shape
    planes, steps = 8, 4
    weight = weight.reshape(planes, -1, half, weight.shape[1])
    blocks = weight.shape[1]
    width = planes * blocks // 2 * weight.shape[3]
    rows = pl.BlockSpec((count, half), lambda i: (0, 0))
    out = pl.BlockSpec((CT, width // steps), lambda i: (0, i))
    return pl.pallas_call(
        project_kernel,
        grid=(steps,),
        in_specs=[
            rows,
            rows,
            pl.BlockSpec((planes // steps,) + weight.shape[1:], lambda i: (i, 0, 0, 0)),
        ],
        out_specs=[out, out],
        out_shape=[
            jax.ShapeDtypeStruct((CT, width), jnp.float32),
            jax.ShapeDtypeStruct((CT, width), jnp.bfloat16),
        ],
        compiler_params=pltpu.CompilerParams(vmem_limit_bytes=32 * 2**20),
        cost_estimate=pl.CostEstimate(flops=1, bytes_accessed=1, transcendentals=0),
        name="project",
    )(mixed_a, mixed_b, weight)


def together(*values):
    return lax.optimization_barrier(values)


def body(
    hidden_states,
    query_weight,
    kv_weight,
    output_weight,
    enc_in_weight,
    enc_out_weight,
    neighbours,
    counts,
    slot_of,
):
    core = lax.axis_index("core")
    plane = lax.axis_index("z")
    feat = neighbours.shape[-1]

    half = enc_in_weight.shape[0] // 2
    sides = [
        lax.dynamic_slice_in_dim(w, core * half, half, 0) for w in (enc_in_weight, enc_out_weight)
    ]
    enc_a = lax.all_gather(jnp.concatenate(sides, axis=0), "z", axis=0, tiled=True)

    def piece_of(weight, steps, axis):
        count = weight.shape[axis] // 8
        index = (plane + own_steps(steps)) % 8
        return lax.dynamic_slice_in_dim(weight, index * count, count, axis)

    width = query_weight.shape[1]
    kv_piece = piece_of(kv_weight, steps_a, 0)
    in_piece = jnp.concatenate(
        [piece_of(query_weight, steps_a, 0), kv_piece[:, 0], kv_piece[:, 1]], axis=0
    )
    out_piece = piece_of(output_weight, steps_b, 1)
    out_piece = jnp.concatenate(
        [out_piece[:, i : i + width] for i in range(0, out_piece.shape[1], width)], axis=0
    )
    normed = rms_normed(hidden_states)

    packed, placing = pack(neighbours, counts, slot_of)
    arrived = lax.all_to_all(packed, ("y", "xh", "core"), split_axis=0, concat_axis=0, tiled=True)
    in_piece = send(in_piece, along_z(steps_a))
    placed = place(arrived, placing)

    placed, in_piece = together(placed, in_piece)
    rows = lax.all_to_all(placed, ("z", "xl"), split_axis=0, concat_axis=0, tiled=True)
    in_piece = send(in_piece, to_member(steps_a))

    rows, in_piece, out_piece, enc_a, normed = together(rows, in_piece, out_piece, enc_a, normed)
    gathered = lax.all_gather(in_piece, "z", axis=0, tiled=True)
    visitors = send(rows, X_OUT)
    enc_b = send(enc_a, CORE)
    out_piece = send(out_piece, along_z(steps_b))
    token_1, token_3 = send(normed, Y_UP[1]), send(normed, Y_UP[3])

    visitors, enc_b, normed = together(visitors, enc_b, normed)
    token_2 = send(normed, Y_UP[2])
    visited = encode(visitors, enc_a, enc_b, keep_raw=False)

    visited, rows, out_piece = together(visited, rows, out_piece)
    returned = send(visited, X_BACK)
    out_piece = send(out_piece, to_member(steps_b))
    encoded = encode(rows, enc_a, enc_b, keep_raw=True)
    encoded = (encoded + returned.astype(jnp.float32)).astype(jnp.bfloat16)

    encoded, normed, token_1, token_2, token_3, out_piece = together(
        encoded, normed, token_1, token_2, token_3, out_piece
    )
    out_pieces = jnp.concatenate([out_piece, send(out_piece, X_OUT)], axis=0)
    out_weight = lax.all_gather(out_pieces, "z", axis=0, tiled=True)
    blocks = [encoded] + [send(encoded, Y_UP[d]) for d in (1, 2, 3)]
    parts = gathered.reshape(8, -1, width)
    q_rows, k_rows = query_weight.shape[0] // 8, feat // 8
    kv_a = jnp.concatenate(
        [
            parts[:, i : i + k_rows].reshape(feat, width)
            for i in (q_rows, q_rows + k_rows)
        ],
        axis=0,
    )
    q_a = parts[:, :q_rows].reshape(-1, width)
    encoded, kv_a, q_a = together(encoded, kv_a, q_a)
    kv_b, q_b = send(kv_a, X_OUT), send(q_a, X_OUT)
    tokens = jnp.concatenate([normed, token_1, token_2, token_3], axis=0)
    tokens = jnp.concatenate([tokens, send(tokens, CORE)], axis=0)
    blocks[0] = encoded
    others = [send(block, CORE) for block in blocks]

    def mix(queries, kv):
        return [attend(d * CT, queries, blocks[d], others[d], kv) for d in range(4)]

    mixed_a = mix(query(tokens, q_a), kv_a)
    mixed_b = mix(query(tokens, q_b), kv_b)

    out_weight, *mixed = together(out_weight, *mixed_a, *mixed_b)
    total = hidden_states.astype(jnp.float32)
    for d in (2, 1, 3, 0):
        near, far = project(mixed[d], mixed[4 + d], out_weight)
        near = near + send(far, CORE).astype(jnp.float32)
        if d:
            near = send(near.astype(jnp.bfloat16), Y_UP[4 - d]).astype(jnp.float32)
        total = total + near
    return total.astype(jnp.bfloat16)


def solution(mesh):
    fine = Mesh(mesh.devices.reshape(SIZES), AXES)
    seq, blk = ("y", "xh", "core"), ("z", "xl")
    placed = (
        P(seq + blk, None),
        P(None, blk),
        P(None, None, blk),
        P(blk, None),
        P(blk, None),
        P(blk, None),
        P(blk, seq, None),
        P(),
        P(),
    )
    return jax.shard_map(
        body, mesh=fine, in_specs=placed, out_specs=P(seq + blk, None), check_vma=False
    )
```

```python
import jax
import jax.numpy as jnp
from jax import lax
from jax.experimental import pallas as pl
from jax.experimental.pallas import tpu as pltpu
from jax.sharding import Mesh, PartitionSpec as P

HD = 128
CT = 64
K_NB = 2
EPS = 1e-06
AXES = ("y", "xh", "core", "z", "xl")
SIZES = (4, 2, 2, 8, 2)


def coords_of(index):
    out = []
    for size in reversed(SIZES):
        out.append(index % size)
        index //= size
    return tuple(reversed(out))


def index_of(coords):
    index = 0
    for size, coord in zip(SIZES, coords):
        index = index * size + coord % size
    return index


def pairs(target):
    count = index_of(tuple(s - 1 for s in SIZES)) + 1
    return [(i, index_of(target(*coords_of(i)))) for i in range(count)]


def x_shift(y, xh, core, z, xl, step):
    x = (xh * 2 + xl + step) % 4
    return (y, x // 2, core, z, x % 2)


X_OUT = pairs(lambda y, xh, c, z, xl: x_shift(y, xh, c, z, xl, 1 - 2 * c))
X_BACK = pairs(lambda y, xh, c, z, xl: x_shift(y, xh, c, z, xl, 2 * c - 1))
CORE = pairs(lambda y, xh, c, z, xl: (y, xh, 1 - c, z, xl))
Y_UP = [pairs(lambda y, xh, c, z, xl, d=d: (y + d, xh, c, z, xl)) for d in range(4)]
def steps_a(y, core):
    return (y, 4 if y == 0 else 8 - y)[core]


def steps_b(y, core):
    return ((4 - y) % 4, y + 4)[core]


def along_z(steps):
    return pairs(lambda y, xh, c, z, xl: (y, xh, c, z + steps(y, c), xl))


def to_member(steps):
    def target(y, xh, c, z, xl):
        member = (z - steps(y, c)) % 8
        return (member // 2, xh, member % 2, z, xl)

    return pairs(target)


def own_steps(steps):
    table = [steps(m // 2, m % 2) for m in range(8)]
    member = lax.axis_index(("y", "core"))
    return sum(jnp.where(member == m, d, 0) for m, d in enumerate(table))


def send(x, perm):
    return lax.ppermute(x, AXES, perm)


def rms_normed(rows):
    widened = rows.astype(jnp.float32)
    inv_rms = lax.rsqrt(jnp.mean(widened * widened, axis=-1, keepdims=True) + EPS)
    return (widened * inv_rms).astype(jnp.bfloat16)


def routing(counts, slot_of, slot_count):
    total_rows = slot_of.shape[0]
    numbers = jnp.arange(total_rows, dtype=jnp.int32)
    run_ends = jnp.cumsum(counts)
    starts = run_ends - counts
    sender = jnp.sum((run_ends[None, :] <= numbers[:, None]).astype(jnp.int32), axis=1)
    holder_ids = jnp.arange(counts.shape[0], dtype=jnp.int32)
    own_start = jnp.sum(
        jnp.where(sender[:, None] == holder_ids[None, :], starts[None, :], 0), axis=1
    )
    position = numbers - own_start
    owners = slot_of // slot_count
    within = slot_of % slot_count
    matches = (
        (sender[:, None] == sender[None, :])
        & (owners[:, None] == owners[None, :])
        & (numbers[None, :] < numbers[:, None])
    )
    ordinal = jnp.sum(matches.astype(jnp.int32), axis=1)
    return (sender, position, owners, within, ordinal)


def pack(neighbours, counts, slot_of):
    seq = ("y", "xh", "core")
    seq_count = 16
    own_index = lax.axis_index(seq)
    tok_dev, capacity, feat = neighbours.shape
    pair_cap = -(-capacity // seq_count)
    slot_count = slot_of.shape[0] // seq_count
    columns = seq_count * pair_cap
    sender, position, owners, within, ordinal = routing(counts, slot_of, slot_count)
    send_col = owners * pair_cap + ordinal
    recv_col = sender * pair_cap + ordinal
    column_ids = jnp.arange(columns, dtype=jnp.int32)
    is_mine = sender == own_index
    pick_send = ((column_ids[:, None] == send_col[None, :]) & is_mine[None, :]).astype(jnp.bfloat16)
    pick_local = (jnp.arange(capacity, dtype=jnp.int32)[:, None] == position[None, :]).astype(
        jnp.bfloat16
    )
    select = jnp.dot(pick_send, pick_local.T, preferred_element_type=jnp.float32)
    is_ours = owners == own_index
    pick_slot = (
        (jnp.arange(slot_count, dtype=jnp.int32)[:, None] == within[None, :]) & is_ours[None, :]
    ).astype(jnp.bfloat16)
    pick_recv = (column_ids[:, None] == recv_col[None, :]).astype(jnp.bfloat16)
    placing = jnp.dot(pick_slot, pick_recv.T, preferred_element_type=jnp.float32)
    packed = jnp.einsum(
        "ki,tid->ktd", select.astype(jnp.bfloat16), neighbours, preferred_element_type=jnp.float32
    ).astype(jnp.bfloat16)
    return packed.reshape(columns * tok_dev, feat), placing.astype(jnp.bfloat16)


def place(arrived, placing):
    slot_count, columns = placing.shape
    placed = jnp.einsum(
        "jc,cr->jr", placing, arrived.reshape(columns, -1), preferred_element_type=jnp.float32
    )
    return placed.astype(jnp.bfloat16).reshape(-1, arrived.shape[1])


def matmul(a, b):
    return jnp.dot(a, b, preferred_element_type=jnp.float32)


def matmul_t(a, b):
    return lax.dot_general(a, b, (((1,), (1,)), ((), ())), preferred_element_type=jnp.float32)


def gelu(x):
    return 0.5 * x * (1.0 + lax.erf(x * (2.0**-0.5)))


def encode_kernel(steps, keep_raw, rows, mine, other, result, normed, total):
    step = pl.program_id(0)

    @pl.when(step == 0)
    def _():
        normed[...] = rms_normed(rows[...])
        total[...] = jnp.zeros_like(total)

    for block in (mine, other):
        parts = [block[i] for i in range(block.shape[0])]
        w_in, w_out = jnp.concatenate(parts[0::2], axis=0), jnp.concatenate(parts[1::2], axis=0)
        units = gelu(matmul_t(normed[...], w_in)).astype(jnp.bfloat16)
        total[...] += matmul(units, w_out)

    @pl.when(step == steps - 1)
    def _():
        summed = total[...]
        if keep_raw:
            summed = summed + rows[...].astype(jnp.float32)
        result[...] = summed.astype(result.dtype)


def encode(rows, mine, other, keep_raw):
    count, feat = rows.shape
    planes = 8
    steps = 4
    mine, other = (w.reshape(2 * planes, -1, feat) for w in (mine, other))
    weight = pl.BlockSpec((2 * planes // steps,) + mine.shape[1:], lambda i: (i, 0, 0))
    whole = pl.BlockSpec((count, feat), lambda i: (0, 0))
    return pl.pallas_call(
        lambda *refs: encode_kernel(steps, keep_raw, *refs),
        grid=(steps,),
        in_specs=[whole, weight, weight],
        out_specs=whole,
        out_shape=jax.ShapeDtypeStruct((count, feat), jnp.float32 if keep_raw else jnp.bfloat16),
        scratch_shapes=[
            pltpu.VMEM((count, feat), jnp.bfloat16),
            pltpu.VMEM((count, feat), jnp.float32),
        ],
        compiler_params=pltpu.CompilerParams(vmem_limit_bytes=32 * 2**20),
        cost_estimate=pl.CostEstimate(flops=1, bytes_accessed=1, transcendentals=0),
        name="encode",
    )(rows, mine, other)


def query_kernel(tokens, weight, result):
    projected = matmul(tokens[...], weight[...])
    result[...] = (projected * HD ** (-0.5)).astype(jnp.bfloat16)


def query(tokens, weight):
    return pl.pallas_call(
        query_kernel,
        out_shape=jax.ShapeDtypeStruct((tokens.shape[0], weight.shape[1]), jnp.bfloat16),
        compiler_params=pltpu.CompilerParams(vmem_limit_bytes=40 * 2**20),
        cost_estimate=pl.CostEstimate(flops=1, bytes_accessed=1, transcendentals=0),
        name="query",
    )(tokens, weight)


def attend_kernel(first, q, enc_0, enc_1, kv, mixed):
    feat = kv.shape[0] // 2
    for span, enc in enumerate((enc_0, enc_1)):
        source = enc[...]
        row = first + span * 4 * CT
        keys = matmul(source, kv[:feat]).astype(jnp.bfloat16)
        values = matmul(source, kv[feat:]).astype(jnp.bfloat16)
        for head in range(2):
            columns = slice(head * HD, (head + 1) * HD)
            scores = matmul_t(q[row : row + CT, columns], keys[:, columns])
            exponent = jnp.exp(scores - jnp.max(scores, axis=-1, keepdims=True))
            probs = exponent / jnp.sum(exponent, axis=-1, keepdims=True)
            out = matmul(probs.astype(jnp.bfloat16), values[:, columns])
            mixed[span * CT : (span + 1) * CT, columns] = out.astype(jnp.bfloat16)


def attend(first, q, enc_0, enc_1, kv):
    return pl.pallas_call(
        lambda *refs: attend_kernel(first, *refs),
        out_shape=jax.ShapeDtypeStruct((2 * CT, q.shape[1]), jnp.bfloat16),
        compiler_params=pltpu.CompilerParams(vmem_limit_bytes=32 * 2**20),
        cost_estimate=pl.CostEstimate(flops=1, bytes_accessed=1, transcendentals=0),
        name="attend",
    )(q, enc_0, enc_1, kv)


def project_kernel(mixed_a, mixed_b, weight, near, far):
    half = mixed_a.shape[1]
    width = weight.shape[3]
    for plane in range(weight.shape[0]):
        for block in range(weight.shape[1] // 2):
            start = (plane * weight.shape[1] // 2 + block) * width
            out = matmul(mixed_a[...], weight[plane, block])
            out = out + matmul(mixed_b[...], weight[plane, weight.shape[1] // 2 + block])
            near[:, start : start + width] = out[:CT]
            far[:, start : start + width] = out[CT:].astype(jnp.bfloat16)


def project(mixed_a, mixed_b, weight):
    count, half = mixed_a.shape
    planes, steps = 8, 4
    weight = weight.reshape(planes, -1, half, weight.shape[1])
    blocks = weight.shape[1]
    width = planes * blocks // 2 * weight.shape[3]
    rows = pl.BlockSpec((count, half), lambda i: (0, 0))
    out = pl.BlockSpec((CT, width // steps), lambda i: (0, i))
    return pl.pallas_call(
        project_kernel,
        grid=(steps,),
        in_specs=[
            rows,
            rows,
            pl.BlockSpec((planes // steps,) + weight.shape[1:], lambda i: (i, 0, 0, 0)),
        ],
        out_specs=[out, out],
        out_shape=[
            jax.ShapeDtypeStruct((CT, width), jnp.float32),
            jax.ShapeDtypeStruct((CT, width), jnp.bfloat16),
        ],
        compiler_params=pltpu.CompilerParams(vmem_limit_bytes=32 * 2**20),
        cost_estimate=pl.CostEstimate(flops=1, bytes_accessed=1, transcendentals=0),
        name="project",
    )(mixed_a, mixed_b, weight)


def together(*values):
    return lax.optimization_barrier(values)


def body(
    hidden_states,
    query_weight,
    kv_weight,
    output_weight,
    enc_in_weight,
    enc_out_weight,
    neighbours,
    counts,
    slot_of,
):
    core = lax.axis_index("core")
    plane = lax.axis_index("z")
    feat = neighbours.shape[-1]

    half = enc_in_weight.shape[0] // 2
    sides = [
        lax.dynamic_slice_in_dim(w, core * half, half, 0) for w in (enc_in_weight, enc_out_weight)
    ]
    enc_a = lax.all_gather(jnp.concatenate(sides, axis=0), "z", axis=0, tiled=True)

    def piece_of(weight, steps, axis):
        count = weight.shape[axis] // 8
        index = (plane + own_steps(steps)) % 8
        return lax.dynamic_slice_in_dim(weight, index * count, count, axis)

    width = query_weight.shape[1]
    kv_piece = piece_of(kv_weight, steps_a, 0)
    in_piece = jnp.concatenate(
        [piece_of(query_weight, steps_a, 0), kv_piece[:, 0], kv_piece[:, 1]], axis=0
    )
    out_piece = piece_of(output_weight, steps_b, 1)
    out_piece = jnp.concatenate(
        [out_piece[:, i : i + width] for i in range(0, out_piece.shape[1], width)], axis=0
    )
    normed = rms_normed(hidden_states)

    packed, placing = pack(neighbours, counts, slot_of)
    arrived = lax.all_to_all(packed, ("y", "xh", "core"), split_axis=0, concat_axis=0, tiled=True)
    in_piece = send(in_piece, along_z(steps_a))
    token_1, token_3 = send(normed, Y_UP[1]), send(normed, Y_UP[3])
    placed = place(arrived, placing)

    placed, in_piece, token_1, token_3 = together(placed, in_piece, token_1, token_3)
    rows = lax.all_to_all(placed, ("z", "xl"), split_axis=0, concat_axis=0, tiled=True)
    in_piece = send(in_piece, to_member(steps_a))

    rows, in_piece, out_piece, enc_a, normed = together(rows, in_piece, out_piece, enc_a, normed)
    gathered = lax.all_gather(in_piece, "z", axis=0, tiled=True)
    visitors = send(rows, X_OUT)
    enc_b = send(enc_a, CORE)
    out_piece = send(out_piece, along_z(steps_b))
    token_2 = send(normed, Y_UP[2])

    visitors, enc_b, out_piece = together(visitors, enc_b, out_piece)
    out_piece = send(out_piece, to_member(steps_b))
    visited = encode(visitors, enc_a, enc_b, keep_raw=False)

    visited, rows, out_piece = together(visited, rows, out_piece)
    returned = send(visited, X_BACK)
    out_pieces = jnp.concatenate([out_piece, send(out_piece, X_OUT)], axis=0)
    encoded = encode(rows, enc_a, enc_b, keep_raw=True)
    encoded = (encoded + returned.astype(jnp.float32)).astype(jnp.bfloat16)

    encoded, normed, token_1, token_2, token_3, out_pieces, gathered = together(
        encoded, normed, token_1, token_2, token_3, out_pieces, gathered
    )
    out_weight = lax.all_gather(out_pieces, "z", axis=0, tiled=True)
    blocks = [encoded] + [send(encoded, Y_UP[d]) for d in (1, 2, 3)]
    parts = gathered.reshape(8, -1, width)
    q_rows, k_rows = query_weight.shape[0] // 8, feat // 8
    kv_a = jnp.concatenate(
        [
            parts[:, i : i + k_rows].reshape(feat, width)
            for i in (q_rows, q_rows + k_rows)
        ],
        axis=0,
    )
    q_a = parts[:, :q_rows].reshape(-1, width)
    kv_b, q_b = send(kv_a, X_OUT), send(q_a, X_OUT)
    tokens = jnp.concatenate([normed, token_1, token_2, token_3], axis=0)
    tokens = jnp.concatenate([tokens, send(tokens, CORE)], axis=0)
    others = [send(block, CORE) for block in blocks]

    def mix(queries, kv):
        return [attend(d * CT, queries, blocks[d], others[d], kv) for d in range(4)]

    mixed_a = mix(query(tokens, q_a), kv_a)
    q_b, *mixed_a = together(q_b, *mixed_a)
    mixed_b = mix(query(tokens, q_b), kv_b)

    out_weight, *mixed = together(out_weight, *mixed_a, *mixed_b)
    total = hidden_states.astype(jnp.float32)
    for d in (2, 1, 3, 0):
        near, far = project(mixed[d], mixed[4 + d], out_weight)
        near = near + send(far, CORE).astype(jnp.float32)
        if d:
            near = send(near.astype(jnp.bfloat16), Y_UP[4 - d]).astype(jnp.float32)
        total = total + near
    return total.astype(jnp.bfloat16)


def solution(mesh):
    fine = Mesh(mesh.devices.reshape(SIZES), AXES)
    seq, blk = ("y", "xh", "core"), ("z", "xl")
    placed = (
        P(seq + blk, None),
        P(None, blk),
        P(None, None, blk),
        P(blk, None),
        P(blk, None),
        P(blk, None),
        P(blk, seq, None),
        P(),
        P(),
    )
    return jax.shard_map(
        body, mesh=fine, in_specs=placed, out_specs=P(seq + blk, None), check_vma=False
    )
```

```python
import jax
import jax.numpy as jnp
from jax import lax
from jax.experimental import pallas as pl
from jax.experimental.pallas import tpu as pltpu
from jax.sharding import Mesh, PartitionSpec as P

HD = 128
CT = 64
K_NB = 2
EPS = 1e-06
AXES = ("y", "xh", "core", "z", "xl")
SIZES = (4, 2, 2, 8, 2)


def coords_of(index):
    out = []
    for size in reversed(SIZES):
        out.append(index % size)
        index //= size
    return tuple(reversed(out))


def index_of(coords):
    index = 0
    for size, coord in zip(SIZES, coords):
        index = index * size + coord % size
    return index


def pairs(target):
    count = index_of(tuple(s - 1 for s in SIZES)) + 1
    return [(i, index_of(target(*coords_of(i)))) for i in range(count)]


def x_shift(y, xh, core, z, xl, step):
    x = (xh * 2 + xl + step) % 4
    return (y, x // 2, core, z, x % 2)


X_OUT = pairs(lambda y, xh, c, z, xl: x_shift(y, xh, c, z, xl, 1 - 2 * c))
X_BACK = pairs(lambda y, xh, c, z, xl: x_shift(y, xh, c, z, xl, 2 * c - 1))
CORE = pairs(lambda y, xh, c, z, xl: (y, xh, 1 - c, z, xl))
Y_UP = [pairs(lambda y, xh, c, z, xl, d=d: (y + d, xh, c, z, xl)) for d in range(4)]
def steps_a(y, core):
    return (y, 4 if y == 0 else 8 - y)[core]


def steps_b(y, core):
    return ((4 - y) % 4, y + 4)[core]


def along_z(steps):
    return pairs(lambda y, xh, c, z, xl: (y, xh, c, z + steps(y, c), xl))


def to_member(steps):
    def target(y, xh, c, z, xl):
        member = (z - steps(y, c)) % 8
        return (member // 2, xh, member % 2, z, xl)

    return pairs(target)


def own_steps(steps):
    table = [steps(m // 2, m % 2) for m in range(8)]
    member = lax.axis_index(("y", "core"))
    return sum(jnp.where(member == m, d, 0) for m, d in enumerate(table))


def send(x, perm):
    return lax.ppermute(x, AXES, perm)


def rms_normed(rows):
    widened = rows.astype(jnp.float32)
    inv_rms = lax.rsqrt(jnp.mean(widened * widened, axis=-1, keepdims=True) + EPS)
    return (widened * inv_rms).astype(jnp.bfloat16)


def routing(counts, slot_of, slot_count):
    total_rows = slot_of.shape[0]
    numbers = jnp.arange(total_rows, dtype=jnp.int32)
    run_ends = jnp.cumsum(counts)
    starts = run_ends - counts
    sender = jnp.sum((run_ends[None, :] <= numbers[:, None]).astype(jnp.int32), axis=1)
    holder_ids = jnp.arange(counts.shape[0], dtype=jnp.int32)
    own_start = jnp.sum(
        jnp.where(sender[:, None] == holder_ids[None, :], starts[None, :], 0), axis=1
    )
    position = numbers - own_start
    owners = slot_of // slot_count
    within = slot_of % slot_count
    matches = (
        (sender[:, None] == sender[None, :])
        & (owners[:, None] == owners[None, :])
        & (numbers[None, :] < numbers[:, None])
    )
    ordinal = jnp.sum(matches.astype(jnp.int32), axis=1)
    return (sender, position, owners, within, ordinal)


def pack(neighbours, counts, slot_of):
    seq = ("y", "xh", "core")
    seq_count = 16
    own_index = lax.axis_index(seq)
    tok_dev, capacity, feat = neighbours.shape
    pair_cap = -(-capacity // seq_count)
    slot_count = slot_of.shape[0] // seq_count
    columns = seq_count * pair_cap
    sender, position, owners, within, ordinal = routing(counts, slot_of, slot_count)
    send_col = owners * pair_cap + ordinal
    recv_col = sender * pair_cap + ordinal
    column_ids = jnp.arange(columns, dtype=jnp.int32)
    is_mine = sender == own_index
    pick_send = ((column_ids[:, None] == send_col[None, :]) & is_mine[None, :]).astype(jnp.bfloat16)
    pick_local = (jnp.arange(capacity, dtype=jnp.int32)[:, None] == position[None, :]).astype(
        jnp.bfloat16
    )
    select = jnp.dot(pick_send, pick_local.T, preferred_element_type=jnp.float32)
    is_ours = owners == own_index
    pick_slot = (
        (jnp.arange(slot_count, dtype=jnp.int32)[:, None] == within[None, :]) & is_ours[None, :]
    ).astype(jnp.bfloat16)
    pick_recv = (column_ids[:, None] == recv_col[None, :]).astype(jnp.bfloat16)
    placing = jnp.dot(pick_slot, pick_recv.T, preferred_element_type=jnp.float32)
    packed = jnp.einsum(
        "ki,tid->ktd", select.astype(jnp.bfloat16), neighbours, preferred_element_type=jnp.float32
    ).astype(jnp.bfloat16)
    return packed.reshape(columns * tok_dev, feat), placing.astype(jnp.bfloat16)


def place(arrived, placing):
    slot_count, columns = placing.shape
    placed = jnp.einsum(
        "jc,cr->jr", placing, arrived.reshape(columns, -1), preferred_element_type=jnp.float32
    )
    return placed.astype(jnp.bfloat16).reshape(-1, arrived.shape[1])


def matmul(a, b):
    return jnp.dot(a, b, preferred_element_type=jnp.float32)


def matmul_t(a, b):
    return lax.dot_general(a, b, (((1,), (1,)), ((), ())), preferred_element_type=jnp.float32)


def gelu(x):
    return 0.5 * x * (1.0 + lax.erf(x * (2.0**-0.5)))


def encode_kernel(steps, keep_raw, rows, mine, other, result, normed, total):
    step = pl.program_id(0)

    @pl.when(step == 0)
    def _():
        normed[...] = rms_normed(rows[...])
        total[...] = jnp.zeros_like(total)

    for block in (mine, other):
        parts = [block[i] for i in range(block.shape[0])]
        w_in, w_out = jnp.concatenate(parts[0::2], axis=0), jnp.concatenate(parts[1::2], axis=0)
        units = gelu(matmul_t(normed[...], w_in)).astype(jnp.bfloat16)
        total[...] += matmul(units, w_out)

    @pl.when(step == steps - 1)
    def _():
        summed = total[...]
        if keep_raw:
            summed = summed + rows[...].astype(jnp.float32)
        result[...] = summed.astype(result.dtype)


def encode(rows, mine, other, keep_raw):
    count, feat = rows.shape
    planes = 8
    steps = 4
    mine, other = (w.reshape(2 * planes, -1, feat) for w in (mine, other))
    weight = pl.BlockSpec((2 * planes // steps,) + mine.shape[1:], lambda i: (i, 0, 0))
    whole = pl.BlockSpec((count, feat), lambda i: (0, 0))
    return pl.pallas_call(
        lambda *refs: encode_kernel(steps, keep_raw, *refs),
        grid=(steps,),
        in_specs=[whole, weight, weight],
        out_specs=whole,
        out_shape=jax.ShapeDtypeStruct((count, feat), jnp.float32 if keep_raw else jnp.bfloat16),
        scratch_shapes=[
            pltpu.VMEM((count, feat), jnp.bfloat16),
            pltpu.VMEM((count, feat), jnp.float32),
        ],
        compiler_params=pltpu.CompilerParams(vmem_limit_bytes=32 * 2**20),
        cost_estimate=pl.CostEstimate(flops=1, bytes_accessed=1, transcendentals=0),
        name="encode",
    )(rows, mine, other)


def query_kernel(tokens, weight, result):
    projected = matmul(tokens[...], weight[...])
    result[...] = (projected * HD ** (-0.5)).astype(jnp.bfloat16)


def query(tokens, weight):
    return pl.pallas_call(
        query_kernel,
        out_shape=jax.ShapeDtypeStruct((tokens.shape[0], weight.shape[1]), jnp.bfloat16),
        compiler_params=pltpu.CompilerParams(vmem_limit_bytes=40 * 2**20),
        cost_estimate=pl.CostEstimate(flops=1, bytes_accessed=1, transcendentals=0),
        name="query",
    )(tokens, weight)


def attend_kernel(first, q, enc_0, enc_1, kv, mixed):
    feat = kv.shape[0] // 2
    for span, enc in enumerate((enc_0, enc_1)):
        source = enc[...]
        row = first + span * 4 * CT
        keys = matmul(source, kv[:feat]).astype(jnp.bfloat16)
        values = matmul(source, kv[feat:]).astype(jnp.bfloat16)
        for head in range(2):
            columns = slice(head * HD, (head + 1) * HD)
            scores = matmul_t(q[row : row + CT, columns], keys[:, columns])
            exponent = jnp.exp(scores - jnp.max(scores, axis=-1, keepdims=True))
            probs = exponent / jnp.sum(exponent, axis=-1, keepdims=True)
            out = matmul(probs.astype(jnp.bfloat16), values[:, columns])
            mixed[span * CT : (span + 1) * CT, columns] = out.astype(jnp.bfloat16)


def attend(first, q, enc_0, enc_1, kv):
    return pl.pallas_call(
        lambda *refs: attend_kernel(first, *refs),
        out_shape=jax.ShapeDtypeStruct((2 * CT, q.shape[1]), jnp.bfloat16),
        compiler_params=pltpu.CompilerParams(vmem_limit_bytes=32 * 2**20),
        cost_estimate=pl.CostEstimate(flops=1, bytes_accessed=1, transcendentals=0),
        name="attend",
    )(q, enc_0, enc_1, kv)


def project_kernel(mixed_a, mixed_b, weight, near, far):
    half = mixed_a.shape[1]
    width = weight.shape[3]
    for plane in range(weight.shape[0]):
        for block in range(weight.shape[1] // 2):
            start = (plane * weight.shape[1] // 2 + block) * width
            out = matmul(mixed_a[...], weight[plane, block])
            out = out + matmul(mixed_b[...], weight[plane, weight.shape[1] // 2 + block])
            near[:, start : start + width] = out[:CT]
            far[:, start : start + width] = out[CT:].astype(jnp.bfloat16)


def project(mixed_a, mixed_b, weight):
    count, half = mixed_a.shape
    planes, steps = 8, 4
    weight = weight.reshape(planes, -1, half, weight.shape[1])
    blocks = weight.shape[1]
    width = planes * blocks // 2 * weight.shape[3]
    rows = pl.BlockSpec((count, half), lambda i: (0, 0))
    out = pl.BlockSpec((CT, width // steps), lambda i: (0, i))
    return pl.pallas_call(
        project_kernel,
        grid=(steps,),
        in_specs=[
            rows,
            rows,
            pl.BlockSpec((planes // steps,) + weight.shape[1:], lambda i: (i, 0, 0, 0)),
        ],
        out_specs=[out, out],
        out_shape=[
            jax.ShapeDtypeStruct((CT, width), jnp.float32),
            jax.ShapeDtypeStruct((CT, width), jnp.bfloat16),
        ],
        compiler_params=pltpu.CompilerParams(vmem_limit_bytes=32 * 2**20),
        cost_estimate=pl.CostEstimate(flops=1, bytes_accessed=1, transcendentals=0),
        name="project",
    )(mixed_a, mixed_b, weight)


def together(*values):
    return lax.optimization_barrier(values)


def body(
    hidden_states,
    query_weight,
    kv_weight,
    output_weight,
    enc_in_weight,
    enc_out_weight,
    neighbours,
    counts,
    slot_of,
):
    core = lax.axis_index("core")
    plane = lax.axis_index("z")
    feat = neighbours.shape[-1]

    half = enc_in_weight.shape[0] // 2
    sides = [
        lax.dynamic_slice_in_dim(w, core * half, half, 0) for w in (enc_in_weight, enc_out_weight)
    ]
    enc_a = lax.all_gather(jnp.concatenate(sides, axis=0), "z", axis=0, tiled=True)

    def piece_of(weight, steps, axis):
        count = weight.shape[axis] // 8
        index = (plane + own_steps(steps)) % 8
        return lax.dynamic_slice_in_dim(weight, index * count, count, axis)

    width = query_weight.shape[1]
    kv_piece = piece_of(kv_weight, steps_a, 0)
    in_piece = jnp.concatenate(
        [piece_of(query_weight, steps_a, 0), kv_piece[:, 0], kv_piece[:, 1]], axis=0
    )
    out_piece = piece_of(output_weight, steps_b, 1)
    out_piece = jnp.concatenate(
        [out_piece[:, i : i + width] for i in range(0, out_piece.shape[1], width)], axis=0
    )
    normed = rms_normed(hidden_states)

    in_piece = send(in_piece, along_z(steps_a))
    packed, placing = pack(neighbours, counts, slot_of)

    packed, in_piece, out_piece = together(packed, in_piece, out_piece)
    arrived = lax.all_to_all(packed, ("y", "xh", "core"), split_axis=0, concat_axis=0, tiled=True)
    in_piece = send(in_piece, to_member(steps_a))
    out_piece = send(out_piece, along_z(steps_b))
    placed = place(arrived, placing)

    placed, in_piece, out_piece, normed = together(placed, in_piece, out_piece, normed)
    rows = lax.all_to_all(placed, ("z", "xl"), split_axis=0, concat_axis=0, tiled=True)
    gathered = lax.all_gather(in_piece, "z", axis=0, tiled=True)
    out_piece = send(out_piece, to_member(steps_b))
    token_1, token_3 = send(normed, Y_UP[1]), send(normed, Y_UP[3])

    rows, out_piece, enc_a, normed = together(rows, out_piece, enc_a, normed)
    visitors = send(rows, X_OUT)
    enc_b = send(enc_a, CORE)
    token_2 = send(normed, Y_UP[2])
    out_other = send(out_piece, X_OUT)
    visitors, enc_b, out_piece, out_other = together(visitors, enc_b, out_piece, out_other)
    out_pieces = jnp.concatenate([out_piece, out_other], axis=0)
    out_weight = lax.all_gather(out_pieces, "z", axis=0, tiled=True)
    visited = encode(visitors, enc_a, enc_b, keep_raw=False)

    visited, rows = together(visited, rows)
    returned = send(visited, X_BACK)
    encoded = encode(rows, enc_a, enc_b, keep_raw=True)
    encoded = (encoded + returned.astype(jnp.float32)).astype(jnp.bfloat16)

    encoded, normed, token_1, token_2, token_3, gathered = together(
        encoded, normed, token_1, token_2, token_3, gathered
    )
    blocks = [encoded] + [send(encoded, Y_UP[d]) for d in (1, 2, 3)]
    parts = gathered.reshape(8, -1, width)
    q_rows, k_rows = query_weight.shape[0] // 8, feat // 8
    kv_a = jnp.concatenate(
        [
            parts[:, i : i + k_rows].reshape(feat, width)
            for i in (q_rows, q_rows + k_rows)
        ],
        axis=0,
    )
    q_a = parts[:, :q_rows].reshape(-1, width)
    kv_b, q_b = send(kv_a, X_OUT), send(q_a, X_OUT)
    tokens = jnp.concatenate([normed, token_1, token_2, token_3], axis=0)
    tokens = jnp.concatenate([tokens, send(tokens, CORE)], axis=0)
    others = [send(block, CORE) for block in blocks]

    def mix(queries, kv):
        return [attend(d * CT, queries, blocks[d], others[d], kv) for d in range(4)]

    mixed_a = mix(query(tokens, q_a), kv_a)
    q_b, *mixed_a = together(q_b, *mixed_a)
    mixed_b = mix(query(tokens, q_b), kv_b)

    out_weight, *mixed = together(out_weight, *mixed_a, *mixed_b)
    total = hidden_states.astype(jnp.float32)
    for d in (2, 1, 3, 0):
        near, far = project(mixed[d], mixed[4 + d], out_weight)
        near = near + send(far, CORE).astype(jnp.float32)
        if d:
            near = send(near.astype(jnp.bfloat16), Y_UP[4 - d]).astype(jnp.float32)
        total = total + near
    return total.astype(jnp.bfloat16)


def solution(mesh):
    fine = Mesh(mesh.devices.reshape(SIZES), AXES)
    seq, blk = ("y", "xh", "core"), ("z", "xl")
    placed = (
        P(seq + blk, None),
        P(None, blk),
        P(None, None, blk),
        P(blk, None),
        P(blk, None),
        P(blk, None),
        P(blk, seq, None),
        P(),
        P(),
    )
    return jax.shard_map(
        body, mesh=fine, in_specs=placed, out_specs=P(seq + blk, None), check_vma=False
    )
```

```python
import jax
import jax.numpy as jnp
from jax import lax
from jax.experimental import pallas as pl
from jax.experimental.pallas import tpu as pltpu
from jax.sharding import Mesh, PartitionSpec as P

HD = 128
CT = 64
K_NB = 2
EPS = 1e-06
AXES = ("y", "xh", "core", "z", "xl")
SIZES = (4, 2, 2, 8, 2)


def coords_of(index):
    out = []
    for size in reversed(SIZES):
        out.append(index % size)
        index //= size
    return tuple(reversed(out))


def index_of(coords):
    index = 0
    for size, coord in zip(SIZES, coords):
        index = index * size + coord % size
    return index


def pairs(target):
    count = index_of(tuple(s - 1 for s in SIZES)) + 1
    return [(i, index_of(target(*coords_of(i)))) for i in range(count)]


def x_shift(y, xh, core, z, xl, step):
    x = (xh * 2 + xl + step) % 4
    return (y, x // 2, core, z, x % 2)


X_OUT = pairs(lambda y, xh, c, z, xl: x_shift(y, xh, c, z, xl, 1 - 2 * c))
X_BACK = pairs(lambda y, xh, c, z, xl: x_shift(y, xh, c, z, xl, 2 * c - 1))
CORE = pairs(lambda y, xh, c, z, xl: (y, xh, 1 - c, z, xl))
Y_UP = [pairs(lambda y, xh, c, z, xl, d=d: (y + d, xh, c, z, xl)) for d in range(4)]
def steps_a(y, core):
    return (y, 4 if y == 0 else 8 - y)[core]


def steps_b(y, core):
    return ((4 - y) % 4, y + 4)[core]


def along_z(steps):
    return pairs(lambda y, xh, c, z, xl: (y, xh, c, z + steps(y, c), xl))


def to_member(steps):
    def target(y, xh, c, z, xl):
        member = (z - steps(y, c)) % 8
        return (member // 2, xh, member % 2, z, xl)

    return pairs(target)


def own_steps(steps):
    table = [steps(m // 2, m % 2) for m in range(8)]
    member = lax.axis_index(("y", "core"))
    return sum(jnp.where(member == m, d, 0) for m, d in enumerate(table))


def send(x, perm):
    return lax.ppermute(x, AXES, perm)


def rms_normed(rows):
    widened = rows.astype(jnp.float32)
    inv_rms = lax.rsqrt(jnp.mean(widened * widened, axis=-1, keepdims=True) + EPS)
    return (widened * inv_rms).astype(jnp.bfloat16)


def routing(counts, slot_of, slot_count):
    total_rows = slot_of.shape[0]
    numbers = jnp.arange(total_rows, dtype=jnp.int32)
    run_ends = jnp.cumsum(counts)
    starts = run_ends - counts
    sender = jnp.sum((run_ends[None, :] <= numbers[:, None]).astype(jnp.int32), axis=1)
    holder_ids = jnp.arange(counts.shape[0], dtype=jnp.int32)
    own_start = jnp.sum(
        jnp.where(sender[:, None] == holder_ids[None, :], starts[None, :], 0), axis=1
    )
    position = numbers - own_start
    owners = slot_of // slot_count
    within = slot_of % slot_count
    matches = (
        (sender[:, None] == sender[None, :])
        & (owners[:, None] == owners[None, :])
        & (numbers[None, :] < numbers[:, None])
    )
    ordinal = jnp.sum(matches.astype(jnp.int32), axis=1)
    return (sender, position, owners, within, ordinal)


def pack(neighbours, counts, slot_of):
    seq = ("y", "xh", "core")
    seq_count = 16
    own_index = lax.axis_index(seq)
    tok_dev, capacity, feat = neighbours.shape
    pair_cap = -(-capacity // seq_count)
    slot_count = slot_of.shape[0] // seq_count
    columns = seq_count * pair_cap
    sender, position, owners, within, ordinal = routing(counts, slot_of, slot_count)
    send_col = owners * pair_cap + ordinal
    recv_col = sender * pair_cap + ordinal
    column_ids = jnp.arange(columns, dtype=jnp.int32)
    is_mine = sender == own_index
    pick_send = ((column_ids[:, None] == send_col[None, :]) & is_mine[None, :]).astype(jnp.bfloat16)
    pick_local = (jnp.arange(capacity, dtype=jnp.int32)[:, None] == position[None, :]).astype(
        jnp.bfloat16
    )
    select = jnp.dot(pick_send, pick_local.T, preferred_element_type=jnp.float32)
    is_ours = owners == own_index
    pick_slot = (
        (jnp.arange(slot_count, dtype=jnp.int32)[:, None] == within[None, :]) & is_ours[None, :]
    ).astype(jnp.bfloat16)
    pick_recv = (column_ids[:, None] == recv_col[None, :]).astype(jnp.bfloat16)
    placing = jnp.dot(pick_slot, pick_recv.T, preferred_element_type=jnp.float32)
    packed = jnp.einsum(
        "ki,tid->ktd", select.astype(jnp.bfloat16), neighbours, preferred_element_type=jnp.float32
    ).astype(jnp.bfloat16)
    return packed.reshape(columns * tok_dev, feat), placing.astype(jnp.bfloat16)


def place(arrived, placing):
    slot_count, columns = placing.shape
    placed = jnp.einsum(
        "jc,cr->jr", placing, arrived.reshape(columns, -1), preferred_element_type=jnp.float32
    )
    return placed.astype(jnp.bfloat16).reshape(-1, arrived.shape[1])


def matmul(a, b):
    return jnp.dot(a, b, preferred_element_type=jnp.float32)


def matmul_t(a, b):
    return lax.dot_general(a, b, (((1,), (1,)), ((), ())), preferred_element_type=jnp.float32)


def gelu(x):
    return 0.5 * x * (1.0 + lax.erf(x * (2.0**-0.5)))


def encode_kernel(steps, keep_raw, rows, mine, other, result, normed, total):
    step = pl.program_id(0)

    @pl.when(step == 0)
    def _():
        normed[...] = rms_normed(rows[...])
        total[...] = jnp.zeros_like(total)

    for block in (mine, other):
        parts = [block[i] for i in range(block.shape[0])]
        w_in, w_out = jnp.concatenate(parts[0::2], axis=0), jnp.concatenate(parts[1::2], axis=0)
        units = gelu(matmul_t(normed[...], w_in)).astype(jnp.bfloat16)
        total[...] += matmul(units, w_out)

    @pl.when(step == steps - 1)
    def _():
        summed = total[...]
        if keep_raw:
            summed = summed + rows[...].astype(jnp.float32)
        result[...] = summed.astype(result.dtype)


def encode(rows, mine, other, keep_raw):
    count, feat = rows.shape
    planes = 8
    steps = 4
    mine, other = (w.reshape(2 * planes, -1, feat) for w in (mine, other))
    weight = pl.BlockSpec((2 * planes // steps,) + mine.shape[1:], lambda i: (i, 0, 0))
    whole = pl.BlockSpec((count, feat), lambda i: (0, 0))
    return pl.pallas_call(
        lambda *refs: encode_kernel(steps, keep_raw, *refs),
        grid=(steps,),
        in_specs=[whole, weight, weight],
        out_specs=whole,
        out_shape=jax.ShapeDtypeStruct((count, feat), jnp.float32 if keep_raw else jnp.bfloat16),
        scratch_shapes=[
            pltpu.VMEM((count, feat), jnp.bfloat16),
            pltpu.VMEM((count, feat), jnp.float32),
        ],
        compiler_params=pltpu.CompilerParams(vmem_limit_bytes=32 * 2**20),
        cost_estimate=pl.CostEstimate(flops=1, bytes_accessed=1, transcendentals=0),
        name="encode",
    )(rows, mine, other)


def query_kernel(tokens, weight, result):
    projected = matmul(tokens[...], weight[...])
    result[...] = (projected * HD ** (-0.5)).astype(jnp.bfloat16)


def query(tokens, weight):
    return pl.pallas_call(
        query_kernel,
        out_shape=jax.ShapeDtypeStruct((tokens.shape[0], weight.shape[1]), jnp.bfloat16),
        compiler_params=pltpu.CompilerParams(vmem_limit_bytes=40 * 2**20),
        cost_estimate=pl.CostEstimate(flops=1, bytes_accessed=1, transcendentals=0),
        name="query",
    )(tokens, weight)


def attend_kernel(first, q, enc_0, enc_1, kv, mixed):
    feat = kv.shape[0] // 2
    for span, enc in enumerate((enc_0, enc_1)):
        source = enc[...]
        row = first + span * 4 * CT
        keys = matmul(source, kv[:feat]).astype(jnp.bfloat16)
        values = matmul(source, kv[feat:]).astype(jnp.bfloat16)
        for head in range(2):
            columns = slice(head * HD, (head + 1) * HD)
            scores = matmul_t(q[row : row + CT, columns], keys[:, columns])
            exponent = jnp.exp(scores - jnp.max(scores, axis=-1, keepdims=True))
            probs = exponent / jnp.sum(exponent, axis=-1, keepdims=True)
            out = matmul(probs.astype(jnp.bfloat16), values[:, columns])
            mixed[span * CT : (span + 1) * CT, columns] = out.astype(jnp.bfloat16)


def attend(first, q, enc_0, enc_1, kv):
    return pl.pallas_call(
        lambda *refs: attend_kernel(first, *refs),
        out_shape=jax.ShapeDtypeStruct((2 * CT, q.shape[1]), jnp.bfloat16),
        compiler_params=pltpu.CompilerParams(vmem_limit_bytes=32 * 2**20),
        cost_estimate=pl.CostEstimate(flops=1, bytes_accessed=1, transcendentals=0),
        name="attend",
    )(q, enc_0, enc_1, kv)


def project_kernel(count, *refs):
    mixed, (weight, near, far) = refs[: 2 * count], refs[2 * count :]
    sides = [
        jnp.concatenate(
            [m[i * CT : (i + 1) * CT] for i in range(2) for m in half], axis=0
        )
        for half in (mixed[:count], mixed[count:])
    ]
    width = weight.shape[3]
    blocks = weight.shape[1] // 2
    for plane in range(weight.shape[0]):
        for block in range(blocks):
            start = (plane * blocks + block) * width
            out = matmul(sides[0], weight[plane, block])
            out = out + matmul(sides[1], weight[plane, blocks + block])
            near[:, start : start + width] = out[: count * CT]
            far[:, start : start + width] = out[count * CT :].astype(jnp.bfloat16)


def project(mixed, weight):
    count = len(mixed) // 2
    half = mixed[0].shape[1]
    planes, steps = 8, 4
    weight = weight.reshape(planes, -1, half, weight.shape[1])
    width = planes * weight.shape[1] // 2 * weight.shape[3]
    out = pl.BlockSpec((count * CT, width // steps), lambda i: (0, i))
    return pl.pallas_call(
        lambda *refs: project_kernel(count, *refs),
        grid=(steps,),
        in_specs=[pl.BlockSpec(m.shape, lambda i: (0, 0)) for m in mixed]
        + [pl.BlockSpec((planes // steps,) + weight.shape[1:], lambda i: (i, 0, 0, 0))],
        out_specs=[out, out],
        out_shape=[
            jax.ShapeDtypeStruct((count * CT, width), jnp.float32),
            jax.ShapeDtypeStruct((count * CT, width), jnp.bfloat16),
        ],
        compiler_params=pltpu.CompilerParams(vmem_limit_bytes=40 * 2**20),
        cost_estimate=pl.CostEstimate(flops=1, bytes_accessed=1, transcendentals=0),
        name="project",
    )(*mixed, weight)


def together(*values):
    return lax.optimization_barrier(values)


def body(
    hidden_states,
    query_weight,
    kv_weight,
    output_weight,
    enc_in_weight,
    enc_out_weight,
    neighbours,
    counts,
    slot_of,
):
    core = lax.axis_index("core")
    plane = lax.axis_index("z")
    feat = neighbours.shape[-1]

    half = enc_in_weight.shape[0] // 2
    sides = [
        lax.dynamic_slice_in_dim(w, core * half, half, 0) for w in (enc_in_weight, enc_out_weight)
    ]
    enc_a = lax.all_gather(jnp.concatenate(sides, axis=0), "z", axis=0, tiled=True)

    def piece_of(weight, steps, axis):
        count = weight.shape[axis] // 8
        index = (plane + own_steps(steps)) % 8
        return lax.dynamic_slice_in_dim(weight, index * count, count, axis)

    width = query_weight.shape[1]
    kv_piece = piece_of(kv_weight, steps_a, 0)
    in_piece = jnp.concatenate(
        [piece_of(query_weight, steps_a, 0), kv_piece[:, 0], kv_piece[:, 1]], axis=0
    )
    out_piece = piece_of(output_weight, steps_b, 1)
    out_piece = jnp.concatenate(
        [out_piece[:, i : i + width] for i in range(0, out_piece.shape[1], width)], axis=0
    )
    normed = rms_normed(hidden_states)

    packed, placing = pack(neighbours, counts, slot_of)
    packed, normed = together(packed, normed)
    arrived = lax.all_to_all(packed, ("y", "xh", "core"), split_axis=0, concat_axis=0, tiled=True)
    in_piece = send(in_piece, along_z(steps_a))
    token_1, token_3 = send(normed, Y_UP[1]), send(normed, Y_UP[3])
    placed = place(arrived, placing)

    placed, in_piece, token_1, token_3 = together(placed, in_piece, token_1, token_3)
    rows = lax.all_to_all(placed, ("z", "xl"), split_axis=0, concat_axis=0, tiled=True)
    in_piece = send(in_piece, to_member(steps_a))

    rows, in_piece, out_piece, enc_a, normed = together(rows, in_piece, out_piece, enc_a, normed)
    gathered = lax.all_gather(in_piece, "z", axis=0, tiled=True)
    visitors = send(rows, X_OUT)
    enc_b = send(enc_a, CORE)
    out_piece = send(out_piece, along_z(steps_b))
    token_2 = send(normed, Y_UP[2])

    visitors, enc_b, out_piece = together(visitors, enc_b, out_piece)
    out_piece = send(out_piece, to_member(steps_b))
    visited = encode(visitors, enc_a, enc_b, keep_raw=False)

    visited, rows, out_piece = together(visited, rows, out_piece)
    returned = send(visited, X_BACK)
    out_pieces = jnp.concatenate([out_piece, send(out_piece, X_OUT)], axis=0)
    encoded = encode(rows, enc_a, enc_b, keep_raw=True)
    encoded = (encoded + returned.astype(jnp.float32)).astype(jnp.bfloat16)

    encoded, normed, token_1, token_2, token_3, out_pieces, gathered = together(
        encoded, normed, token_1, token_2, token_3, out_pieces, gathered
    )
    out_weight = lax.all_gather(out_pieces, "z", axis=0, tiled=True)
    blocks = [encoded] + [send(encoded, Y_UP[d]) for d in (1, 2, 3)]
    parts = gathered.reshape(8, -1, width)
    q_rows, k_rows = query_weight.shape[0] // 8, feat // 8
    kv_a = jnp.concatenate(
        [
            parts[:, i : i + k_rows].reshape(feat, width)
            for i in (q_rows, q_rows + k_rows)
        ],
        axis=0,
    )
    q_a = parts[:, :q_rows].reshape(-1, width)
    kv_b, q_b = send(kv_a, X_OUT), send(q_a, X_OUT)
    tokens = jnp.concatenate([normed, token_1, token_2, token_3], axis=0)
    tokens = jnp.concatenate([tokens, send(tokens, CORE)], axis=0)
    others = [send(block, CORE) for block in blocks]

    def mix(queries, kv):
        return [attend(d * CT, queries, blocks[d], others[d], kv) for d in range(4)]

    mixed_a = mix(query(tokens, q_a), kv_a)
    q_b, *mixed_a = together(q_b, *mixed_a)
    mixed_b = mix(query(tokens, q_b), kv_b)

    out_weight, *mixed = together(out_weight, *mixed_a, *mixed_b)
    near, far = project(mixed, out_weight)
    far = send(far, CORE)
    total = hidden_states.astype(jnp.float32)
    for d in (2, 1, 3, 0):
        rows = slice(d * CT, (d + 1) * CT)
        summed = near[rows] + far[rows].astype(jnp.float32)
        if d:
            summed = send(summed.astype(jnp.bfloat16), Y_UP[4 - d]).astype(jnp.float32)
        total = total + summed
    return total.astype(jnp.bfloat16)


def solution(mesh):
    fine = Mesh(mesh.devices.reshape(SIZES), AXES)
    seq, blk = ("y", "xh", "core"), ("z", "xl")
    placed = (
        P(seq + blk, None),
        P(None, blk),
        P(None, None, blk),
        P(blk, None),
        P(blk, None),
        P(blk, None),
        P(blk, seq, None),
        P(),
        P(),
    )
    return jax.shard_map(
        body, mesh=fine, in_specs=placed, out_specs=P(seq + blk, None), check_vma=False
    )
```
